512 devices in a mesh: row: 8 (over z_lo), col: 8 (over y, core), depth: 8 (over z_hi, x).
Axes of the slice: x: 4, y: 4, z: 16 (z_hi: 2, z_lo: 8; z = z_hi * 8 + z_lo), core: 2. Of those that a mesh axis runs over, the one named last changes fastest.
Arguments:
- tokens: bfloat16 [2048, 4096], P(('row', 'depth'), 'col'), may hold values from -6 to 6
- gate_weight: bfloat16 [4096, 14336], P('row', 'col'), may hold values from -0.09375 to 0.09375
- up_weight: bfloat16 [4096, 14336], P('row', 'col'), may hold values from -0.09375 to 0.09375
- grad_hidden: bfloat16 [2048, 14336], P(('row', 'depth'), 'col'), may hold values from -6 to 6
Outputs:
- hidden: bfloat16 [2048, 14336], P(('row', 'depth'), 'col')
- grad_tokens: bfloat16 [2048, 4096], P(('col', 'depth'), 'row')
- grad_gate_weight: float32 [4096, 14336], P('row', ('col', 'depth'))
- grad_up_weight: float32 [4096, 14336], P('row', ('col', 'depth'))
The draws below stay inside these ranges and needn't reach their ends.
All inputs are finite; a program needn't handle non-finite values.
Results may differ from the reference program's by a relative error of at most 0.028.
Values may be sent and summed in bfloat16 or wider, within the bound.
No kernel may reach another device: no remote copies, remote signals or barrier semaphores. Data moves between devices by JAX's collectives and lax.ppermute only.
A program may use at most 64 MiB of HBM per device.

```python
import jax
import jax.numpy as jnp
from jax import lax

D = 4096
FF = 14336
TOKENS = 2048
N_ROW = 8
N_COL = 8


def levels(stream_key, shape, split, least, top_value):
    level, own = 1.0, jax.random.fold_in(stream_key, 6)
    for axis_at, blocks in split:
        steps = jnp.exp(jax.random.uniform(jax.random.fold_in(own, axis_at), (blocks,), jnp.float32, least / len(split), top_value / len(split)))
        level = level * jnp.repeat(steps, shape[axis_at] // blocks).reshape([-1 if axis == axis_at else 1 for axis in range(len(shape))])
    return level


def noise(stream_key, shape, width, most, shards=(), dtype=jnp.bfloat16):
    gain = levels(stream_key, shape, shards, -0.22, 0.18) if shards else 1.0
    values = jax.random.normal(stream_key, shape, jnp.float32) * width * gain
    return jnp.minimum(jnp.maximum(values, -most), most).astype(dtype)


def setup_inputs(seed: int = 0) -> dict:
    arg_keys = jax.random.split(jax.random.key(seed), 5)
    tokens = noise(arg_keys[0], (TOKENS, D), 1.0, 6.0, ((0, 64), (1, 8)))
    gate_weight = noise(arg_keys[1], (D, FF), D ** -0.5, 0.09375, ((0, 8), (1, 8)))
    up_weight = noise(arg_keys[2], (D, FF), D ** -0.5, 0.09375, ((0, 8), (1, 8)))
    grad_hidden = noise(arg_keys[3], (TOKENS, FF), 1.0, 6.0, ((0, 64), (1, 8)))
    return dict(tokens=tokens, gate_weight=gate_weight, up_weight=up_weight, grad_hidden=grad_hidden)


def local_grads(gate_pre, up_pre, cotangent):
    sigmoid_gate = jax.nn.sigmoid(gate_pre)
    cotan_f32 = cotangent.astype(jnp.float32)
    grad_gate = (cotan_f32 * up_pre * sigmoid_gate * (1.0 + gate_pre * (1.0 - sigmoid_gate))).astype(jnp.bfloat16)
    grad_up = (cotan_f32 * jax.nn.silu(gate_pre)).astype(jnp.bfloat16)
    return grad_gate, grad_up


def reference(tokens, gate_weight, up_weight, grad_hidden):
    feature_block = D // N_ROW
    gate_pre = jnp.zeros((tokens.shape[0], FF), jnp.float32)
    up_pre = jnp.zeros((tokens.shape[0], FF), jnp.float32)
    for block in range(N_ROW):
        first = block * feature_block
        last = first + feature_block
        gate_part = jnp.dot(tokens[:, first:last], gate_weight[first:last, :], preferred_element_type=jnp.float32)
        up_part = jnp.dot(tokens[:, first:last], up_weight[first:last, :], preferred_element_type=jnp.float32)
        gate_round = lax.optimization_barrier(gate_part.astype(jnp.bfloat16))
        up_round = lax.optimization_barrier(up_part.astype(jnp.bfloat16))
        gate_pre = gate_pre + gate_round.astype(jnp.float32)
        up_pre = up_pre + up_round.astype(jnp.float32)
    hidden = (jax.nn.silu(gate_pre) * up_pre).astype(jnp.bfloat16)
    grad_gate, grad_up = local_grads(gate_pre, up_pre, grad_hidden)
    block_cols = FF // N_COL
    total = jnp.zeros((tokens.shape[0], tokens.shape[1]), jnp.float32)
    for block in range(N_COL):
        column_start = block * block_cols
        column_end = column_start + block_cols
        part_sum = jnp.dot(grad_gate[:, column_start:column_end], gate_weight[:, column_start:column_end].T, preferred_element_type=jnp.float32)
        part_sum = part_sum + jnp.dot(grad_up[:, column_start:column_end], up_weight[:, column_start:column_end].T, preferred_element_type=jnp.float32)
        rounded = lax.optimization_barrier(part_sum.astype(jnp.bfloat16))
        total = total + rounded.astype(jnp.float32)
    grad_tokens = total.astype(jnp.bfloat16)
    grad_gate_weight = jnp.dot(tokens.T, grad_gate, preferred_element_type=jnp.float32)
    grad_up_weight = jnp.dot(tokens.T, grad_up, preferred_element_type=jnp.float32)
    return hidden, grad_tokens, grad_gate_weight, grad_up_weight
```

```python
import jax
import jax.numpy as jnp
from jax import lax
from jax.sharding import Mesh, PartitionSpec as P

RING = 16
ROWS = 8
BEFORE = 3


def ring_index(z):
    z %= RING
    return (z % ROWS) * 2 + z // ROWS


def ring_shift(value, step):
    pairs = [(ring_index(z), ring_index(z + step)) for z in range(RING)]
    return lax.ppermute(value, ("r", "h"), pairs)


def place(z, col):
    z %= RING
    return ((z % ROWS) * ROWS + col) * 2 + z // ROWS


def token_pairs():
    pairs = []
    for z in range(RING):
        for offset in range(ROWS):
            pairs.append((place(z + offset - BEFORE, z % ROWS), place(z, offset)))
    return pairs


def result_pairs():
    pairs = []
    for z in range(RING):
        for offset in range(ROWS):
            tile = (z + offset - 4) % RING
            pairs.append((place(z, offset), place(z % ROWS + ROWS * (tile // ROWS), tile % ROWS)))
    return pairs


def dot_f32(left, right, dims):
    return lax.dot_general(left, right, (dims, ((), ())), preferred_element_type=jnp.float32)


def gather_plane(piece):
    copies = jnp.broadcast_to(piece[None], (32,) + piece.shape)
    all_pieces = lax.all_to_all(copies, ("y", "c", "x"), split_axis=0, concat_axis=0, tiled=True)
    return all_pieces.reshape(32 * piece.shape[0], piece.shape[1])


def local(tokens, gate_weight, up_weight, grad_hidden):
    own_x = lax.axis_index("x")
    own_h = lax.axis_index("h")
    features, hidden_cols = gate_weight.shape
    part = hidden_cols // 8

    def own_columns(weight):
        first = lax.dynamic_slice(weight, (0, own_x * part), (features, part))
        second = lax.dynamic_slice(weight, (0, 4 * part + own_x * part), (features, part))
        return [first, second]

    weights = jnp.concatenate(own_columns(gate_weight) + own_columns(up_weight), 1)

    piece = lax.ppermute(tokens, ("r", "y", "c", "h"), token_pairs())
    near_tokens = gather_plane(piece)
    far_tokens = gather_plane(lax.ppermute(piece, "h", [(0, 1), (1, 0)]))

    cotangent = lax.all_to_all(
        grad_hidden.reshape(-1, 2, 4, part), "x", split_axis=2, concat_axis=0, tiled=True
    ).reshape(-1, 2 * part)

    partial = dot_f32(near_tokens, weights, ((1,), (0,))).astype(jnp.bfloat16)
    partial = partial.reshape(ROWS, -1, 4 * part)
    total = partial[BEFORE].astype(jnp.float32)
    arrived = []
    for offset in (7, 0, 6, 1, 5, 2, 4):
        arrived.append(ring_shift(partial[offset], offset - BEFORE))
    for term in arrived:
        total = total + term.astype(jnp.float32)
    gate_pre = total[:, : 2 * part]
    up_pre = total[:, 2 * part :]

    sigmoid = jax.nn.sigmoid(gate_pre)
    silu = gate_pre * sigmoid
    hidden = (silu * up_pre).astype(jnp.bfloat16)
    cotangent = cotangent.astype(jnp.float32)
    grad_gate = (cotangent * up_pre * sigmoid * (1.0 + gate_pre * (1.0 - sigmoid))).astype(jnp.bfloat16)
    grad_up = (cotangent * silu).astype(jnp.bfloat16)
    grads = jnp.concatenate([grad_gate, grad_up], 1)

    hidden = lax.all_to_all(
        hidden.reshape(-1, 2, 1, part), "x", split_axis=0, concat_axis=2, tiled=True
    ).reshape(-1, 8 * part)

    tiles = {0: grads}
    right = left = grads
    for step in range(1, 9):
        right = ring_shift(right, 1)
        tiles[-step] = right
        if step < 8:
            left = ring_shift(left, -1)
            tiles[step] = left

    reach = jnp.concatenate([tiles[offset] for offset in range(-4, 4)], 0)
    terms = dot_f32(reach, weights, ((1,), (1,))).astype(jnp.bfloat16)
    terms = lax.all_to_all(
        terms.reshape(32, -1, features), ("y", "c", "x"), split_axis=0, concat_axis=0, tiled=True
    )
    grad_tokens = jnp.sum(terms.astype(jnp.float32), 0).astype(jnp.bfloat16)
    grad_tokens = lax.ppermute(grad_tokens, ("r", "y", "c", "h"), result_pairs())

    def own_half(offsets):
        both = jnp.concatenate([tiles[offset] for offset in offsets], 0)
        low = jnp.concatenate([both[:, :part], both[:, 2 * part : 3 * part]], 1)
        high = jnp.concatenate([both[:, part : 2 * part], both[:, 3 * part :]], 1)
        return jnp.where(own_h == 0, low, high)

    near = own_half(range(-3, 5))
    far = own_half((5, 6, 7, -8, -7, -6, -5, -4))
    weight_grads = dot_f32(near_tokens, near, ((0,), (0,))) + dot_f32(far_tokens, far, ((0,), (0,)))
    return hidden, grad_tokens, weight_grads[:, :part], weight_grads[:, part:]


def solution(mesh):
    fine = Mesh(mesh.devices.reshape(8, 4, 2, 2, 4), ("r", "y", "c", "h", "x"))
    return jax.shard_map(
        local,
        mesh=fine,
        in_specs=(
            P(("r", "h", "x"), ("y", "c")),
            P("r", ("y", "c")),
            P("r", ("y", "c")),
            P(("r", "h", "x"), ("y", "c")),
        ),
        out_specs=(
            P(("r", "h", "x"), ("y", "c")),
            P(("y", "c", "h", "x"), "r"),
            P("r", ("y", "c", "h", "x")),
            P("r", ("y", "c", "h", "x")),
        ),
        check_vma=False,
    )
```

```python
import jax
import jax.numpy as jnp
from jax import lax
from jax.experimental import pallas as pl
from jax.experimental.pallas import tpu as pltpu
from jax.sharding import Mesh, PartitionSpec as P

RING = 16
ROWS = 8
BEFORE = 3


def ring_index(z):
    z %= RING
    return (z % ROWS) * 2 + z // ROWS


def ring_shift(value, step):
    pairs = [(ring_index(z), ring_index(z + step)) for z in range(RING)]
    return lax.ppermute(value, ("r", "h"), pairs)


def place(z, col):
    z %= RING
    return ((z % ROWS) * ROWS + col) * 2 + z // ROWS


def token_pairs():
    pairs = []
    for z in range(RING):
        for offset in range(ROWS):
            pairs.append((place(z + offset - BEFORE, z % ROWS), place(z, offset)))
    return pairs


def result_pairs():
    pairs = []
    for z in range(RING):
        for offset in range(ROWS):
            tile = (z + offset - 4) % RING
            pairs.append((place(z, offset), place(z % ROWS + ROWS * (tile // ROWS), tile % ROWS)))
    return pairs


def dot_f32(left, right, dims=((1,), (0,))):
    return lax.dot_general(left, right, (dims, ((), ())), preferred_element_type=jnp.float32)


def gather_plane(piece):
    copies = jnp.broadcast_to(piece[None], (32,) + piece.shape)
    all_pieces = lax.all_to_all(copies, ("y", "c", "x"), split_axis=0, concat_axis=0, tiled=True)
    return all_pieces.reshape(32 * piece.shape[0], piece.shape[1])


def forward_kernel(tokens_ref, weights_ref, *tile_refs):
    for at, tile_ref in enumerate(tile_refs):
        product = dot_f32(tokens_ref[at * 128 : (at + 1) * 128, :], weights_ref[...])
        tile_ref[...] = product.T.astype(jnp.bfloat16)


def forward_tiles(tokens, weights):
    cols = weights.shape[1]
    return pl.pallas_call(
        forward_kernel,
        out_shape=[jax.ShapeDtypeStruct((cols, 128), jnp.bfloat16)] * ROWS,
        compiler_params=pltpu.CompilerParams(vmem_limit_bytes=32 << 20),
    )(tokens, weights)


def terms_kernel(weights_ref, *refs):
    out_ref = refs[-1]
    for at, tile_ref in enumerate(refs[:-1]):
        product = dot_f32(weights_ref[...], tile_ref[...])
        out_ref[at * 128 : (at + 1) * 128, :] = product.T.astype(jnp.bfloat16)


def token_terms(weights, tiles):
    return pl.pallas_call(
        terms_kernel,
        out_shape=jax.ShapeDtypeStruct((128 * len(tiles), weights.shape[0]), jnp.bfloat16),
        compiler_params=pltpu.CompilerParams(vmem_limit_bytes=32 << 20),
    )(weights, *tiles)


def own_half_product(half_ref, tokens_ref, tile_refs, wide_ref):
    rows = wide_ref.shape[0]
    first = pl.multiple_of(half_ref[0] * rows, 16)
    for at, tile_ref in enumerate(tile_refs):
        wide_ref[:, at * 128 : (at + 1) * 128] = tile_ref[pl.ds(first, rows), :]
    return dot_f32(wide_ref[...], tokens_ref[...])


def near_kernel(half_ref, tokens_ref, *refs):
    out_ref, wide_ref = refs[-2:]
    out_ref[...] = own_half_product(half_ref, tokens_ref, refs[:-2], wide_ref)


def far_kernel(half_ref, tokens_ref, near_ref, *refs):
    gate_ref, up_ref, wide_ref = refs[-3:]
    total = near_ref[...] + own_half_product(half_ref, tokens_ref, refs[:-3], wide_ref)
    part = gate_ref.shape[0]
    gate_ref[...] = total[:part, :]
    up_ref[...] = total[part:, :]


SMEM_SPEC = pl.BlockSpec(memory_space=pltpu.SMEM)
VMEM_SPEC = pl.BlockSpec(memory_space=pltpu.VMEM)


def near_product(half, tokens, tiles):
    rows = tiles[0].shape[0] // 2
    return pl.pallas_call(
        near_kernel,
        in_specs=[SMEM_SPEC] + [VMEM_SPEC] * (1 + len(tiles)),
        out_specs=VMEM_SPEC,
        out_shape=jax.ShapeDtypeStruct((rows, tokens.shape[1]), jnp.float32),
        scratch_shapes=[pltpu.VMEM((rows, tokens.shape[0]), jnp.bfloat16)],
        compiler_params=pltpu.CompilerParams(vmem_limit_bytes=32 << 20),
    )(half, tokens, *tiles)


def far_product(half, tokens, near, tiles):
    rows = tiles[0].shape[0] // 2
    return pl.pallas_call(
        far_kernel,
        in_specs=[SMEM_SPEC] + [VMEM_SPEC] * (2 + len(tiles)),
        out_specs=[VMEM_SPEC] * 2,
        out_shape=[jax.ShapeDtypeStruct((rows // 2, tokens.shape[1]), jnp.float32)] * 2,
        scratch_shapes=[pltpu.VMEM((rows, tokens.shape[0]), jnp.bfloat16)],
        compiler_params=pltpu.CompilerParams(vmem_limit_bytes=32 << 20),
    )(half, tokens, near, *tiles)


def local(tokens, gate_weight, up_weight, grad_hidden):
    own_x = lax.axis_index("x")
    half = lax.axis_index("h").astype(jnp.int32).reshape(1)
    features, hidden_cols = gate_weight.shape
    part = hidden_cols // 8

    def own_columns(weight, which):
        return lax.dynamic_slice(weight, (0, (which * 4 + own_x) * part), (features, part))

    weights = jnp.concatenate(
        [own_columns(weight, which) for which in (0, 1) for weight in (gate_weight, up_weight)], 1
    )

    piece = lax.ppermute(tokens, ("r", "y", "c", "h"), token_pairs())
    cotangent = lax.all_to_all(
        grad_hidden.reshape(-1, 2, 4, part), "x", split_axis=2, concat_axis=0, tiled=True
    )
    piece, cotangent = lax.optimization_barrier((piece, cotangent))
    near_tokens = gather_plane(piece)
    far_piece = lax.ppermute(piece, "h", [(0, 1), (1, 0)])
    near_tokens, far_piece, weights = lax.optimization_barrier((near_tokens, far_piece, weights))
    cotangent = cotangent.reshape(-1, 2 * part).T.astype(jnp.float32)

    partial = forward_tiles(near_tokens, weights)
    far_tokens = gather_plane(far_piece)
    arrived = [partial[BEFORE]]
    for offset in (7, 0, 6, 1, 5, 2, 4):
        arrived.append(ring_shift(partial[offset], offset - BEFORE))
    *arrived, far_tokens = lax.optimization_barrier((*arrived, far_tokens))
    total = arrived[0].astype(jnp.float32)
    for term in arrived[1:]:
        total = total + term.astype(jnp.float32)
    gate_pre = jnp.concatenate([total[:part], total[2 * part : 3 * part]], 0)
    up_pre = jnp.concatenate([total[part : 2 * part], total[3 * part :]], 0)

    sigmoid = jax.nn.sigmoid(gate_pre)
    silu = gate_pre * sigmoid
    hidden = (silu * up_pre).astype(jnp.bfloat16)
    grad_gate = (cotangent * up_pre * sigmoid * (1.0 + gate_pre * (1.0 - sigmoid))).astype(jnp.bfloat16)
    grad_up = (cotangent * silu).astype(jnp.bfloat16)
    grads = jnp.concatenate([grad_gate[:part], grad_up[:part], grad_gate[part:], grad_up[part:]], 0)

    hidden = lax.all_to_all(
        hidden.T.reshape(-1, 2, 1, part), "x", split_axis=0, concat_axis=2, tiled=True
    )

    tiles = {0: grads}
    right = left = grads
    for step in range(1, 9):
        right = ring_shift(right, 1)
        tiles[-step] = right
        if step < 8:
            left = ring_shift(left, -1)
            tiles[step] = left
        if step == 4:
            terms = token_terms(weights, [tiles[offset] for offset in range(-4, 4)])
            right, left, terms, hidden = lax.optimization_barrier((right, left, terms, hidden))
            terms = lax.all_to_all(
                terms.reshape(32, -1, features), ("y", "c", "x"), split_axis=0, concat_axis=0, tiled=True
            )
            near = near_product(half, near_tokens, [tiles[offset] for offset in range(-3, 5)])
        if step == 6:
            right, left, terms = lax.optimization_barrier((right, left, terms))
            grad_tokens = jnp.sum(terms.astype(jnp.float32), 0).astype(jnp.bfloat16)
            right, left, grad_tokens = lax.optimization_barrier((right, left, grad_tokens))
            grad_tokens = lax.ppermute(grad_tokens, ("r", "y", "c", "h"), result_pairs())

    far_tiles = [tiles[offset] for offset in (5, 6, 7, -8, -7, -6, -5, -4)]
    gate_grad, up_grad = far_product(half, far_tokens, near, far_tiles)
    return hidden.reshape(-1, hidden_cols), grad_tokens, gate_grad.T, up_grad.T


def solution(mesh):
    fine = Mesh(mesh.devices.reshape(8, 4, 2, 2, 4), ("r", "y", "c", "h", "x"))
    return jax.shard_map(
        local,
        mesh=fine,
        in_specs=(
            P(("r", "h", "x"), ("y", "c")),
            P("r", ("y", "c")),
            P("r", ("y", "c")),
            P(("r", "h", "x"), ("y", "c")),
        ),
        out_specs=(
            P(("r", "h", "x"), ("y", "c")),
            P(("y", "c", "h", "x"), "r"),
            P("r", ("y", "c", "h", "x")),
            P("r", ("y", "c", "h", "x")),
        ),
        check_vma=False,
    )
```

```python
import functools

import jax
import jax.numpy as jnp
from jax import lax
from jax.experimental import pallas as pl
from jax.experimental.pallas import tpu as pltpu
from jax.sharding import Mesh, PartitionSpec as P

RING = 16
ROWS = 8
BEFORE = 3


def ring_index(z):
    z %= RING
    return (z % ROWS) * 2 + z // ROWS


def ring_shift(value, step):
    pairs = [(ring_index(z), ring_index(z + step)) for z in range(RING)]
    return lax.ppermute(value, ("r", "h"), pairs)


def place(z, col):
    z %= RING
    return ((z % ROWS) * ROWS + col) * 2 + z // ROWS


def slot(offset):
    return (offset % 4) * 2 + offset // 4


def token_pairs():
    pairs = []
    for z in range(RING):
        for offset in range(ROWS):
            pairs.append((place(z + offset - BEFORE, z % ROWS), place(z, slot(offset))))
    return pairs


def result_pairs():
    pairs = []
    for z in range(RING):
        for offset in range(ROWS):
            tile = (z + offset - BEFORE) % RING
            pairs.append((place(z, slot(offset)), place(z % ROWS + ROWS * (tile // ROWS), tile % ROWS)))
    return pairs


def dot_f32(left, right, dims=((1,), (0,))):
    return lax.dot_general(left, right, (dims, ((), ())), preferred_element_type=jnp.float32)


SMEM_SPEC = pl.BlockSpec(memory_space=pltpu.SMEM)
VMEM_SPEC = pl.BlockSpec(memory_space=pltpu.VMEM)
PARAMS = pltpu.CompilerParams(vmem_limit_bytes=32 << 20)


def swap_cores(value):
    return lax.ppermute(value, "c", [(0, 1), (1, 0)])


def join_cores(core, own_ref, other_ref, both_ref):
    rows = own_ref.shape[0]
    both_ref[pl.ds(pl.multiple_of(core * rows, rows), rows), :] = own_ref[...]
    both_ref[pl.ds(pl.multiple_of((1 - core) * rows, rows), rows), :] = other_ref[...]


def forward_kernel(offsets, core_ref, own_ref, other_ref, weights_ref, *refs):
    tokens_ref = refs[-1]
    join_cores(core_ref[0], own_ref, other_ref, tokens_ref)
    for offset, tile_ref in zip(offsets, refs):
        product = dot_f32(tokens_ref[offset * 128 : (offset + 1) * 128, :], weights_ref[...])
        tile_ref[...] = product.T.astype(jnp.bfloat16)


def forward_tiles(offsets, core, own, other, weights):
    features, cols = weights.shape
    return pl.pallas_call(
        functools.partial(forward_kernel, offsets),
        in_specs=[SMEM_SPEC] + [VMEM_SPEC] * 3,
        out_specs=[VMEM_SPEC] * len(offsets),
        out_shape=[jax.ShapeDtypeStruct((cols, 128), jnp.bfloat16)] * len(offsets),
        scratch_shapes=[pltpu.VMEM((ROWS * 128, features), jnp.bfloat16)],
        compiler_params=PARAMS,
    )(core, own, other, weights)


def terms_kernel(core_ref, weights_ref, *refs):
    tile_refs = refs[:ROWS]
    keep_ref, send_ref, all_ref = refs[ROWS:]
    for at, tile_ref in enumerate(tile_refs):
        product = dot_f32(weights_ref[...], tile_ref[...])
        all_ref[at * 128 : (at + 1) * 128, :] = product.T
    rows = keep_ref.shape[0]
    core = core_ref[0]
    keep_ref[...] = all_ref[pl.ds(pl.multiple_of(core * rows, rows), rows), :]
    send = all_ref[pl.ds(pl.multiple_of((1 - core) * rows, rows), rows), :]
    send_ref[...] = send.astype(jnp.bfloat16)


def token_terms(core, weights, tiles):
    shape = (ROWS * 64, weights.shape[0])
    return pl.pallas_call(
        terms_kernel,
        in_specs=[SMEM_SPEC] + [VMEM_SPEC] * (1 + ROWS),
        out_specs=[VMEM_SPEC] * 2,
        out_shape=[jax.ShapeDtypeStruct(shape, jnp.float32), jax.ShapeDtypeStruct(shape, jnp.bfloat16)],
        scratch_shapes=[pltpu.VMEM((ROWS * 128, shape[1]), jnp.float32)],
        compiler_params=PARAMS,
    )(core, weights, *tiles)


def weight_grad_kernel(core_ref, half_ref, own_ref, other_ref, *refs):
    tile_refs = refs[:ROWS]
    keep_ref, send_ref, tokens_ref, wide_ref = refs[ROWS:]
    join_cores(core_ref[0], own_ref, other_ref, tokens_ref)
    rows = wide_ref.shape[0]

    def product(half):
        first = pl.multiple_of(half * rows, 16)
        for at, tile_ref in enumerate(tile_refs):
            wide_ref[:, at * 128 : (at + 1) * 128] = tile_ref[pl.ds(first, rows), :]
        return dot_f32(wide_ref[...], tokens_ref[...])

    send_ref[...] = product(1 - half_ref[0]).astype(jnp.bfloat16)
    keep_ref[...] = product(half_ref[0])


def weight_grads(core, half, own, other, tiles):
    rows = tiles[0].shape[0] // 2
    features = own.shape[1]
    return pl.pallas_call(
        weight_grad_kernel,
        in_specs=[SMEM_SPEC] * 2 + [VMEM_SPEC] * (2 + ROWS),
        out_specs=[VMEM_SPEC] * 2,
        out_shape=[
            jax.ShapeDtypeStruct((rows, features), jnp.float32),
            jax.ShapeDtypeStruct((rows, features), jnp.bfloat16),
        ],
        scratch_shapes=[
            pltpu.VMEM((ROWS * 128, features), jnp.bfloat16),
            pltpu.VMEM((rows, ROWS * 128), jnp.bfloat16),
        ],
        compiler_params=PARAMS,
    )(core, half, own, other, *tiles)


def add_tiles(left, right):
    return (left.astype(jnp.float32) + right.astype(jnp.float32)).astype(jnp.bfloat16)


def local(tokens, gate_weight, up_weight, grad_hidden):
    own_x = lax.axis_index("x")
    core = lax.axis_index("c").astype(jnp.int32).reshape(1)
    half = lax.axis_index("h").astype(jnp.int32).reshape(1)
    features, hidden_cols = gate_weight.shape
    part = hidden_cols // 8

    def own_columns(weight, which):
        return lax.dynamic_slice(weight, (0, (which * 4 + own_x) * part), (features, part))

    weights = jnp.concatenate(
        [own_columns(weight, which) for which in (0, 1) for weight in (gate_weight, up_weight)], 1
    )

    piece = lax.ppermute(tokens, ("r", "y", "c", "h"), token_pairs())
    piece, grad_hidden = lax.optimization_barrier((piece, grad_hidden))
    copies = jnp.broadcast_to(piece[None], (16,) + piece.shape)
    own_tokens = lax.all_to_all(copies, ("y", "x"), split_axis=0, concat_axis=0, tiled=True)
    own_tokens = own_tokens.reshape(-1, features)
    cotangent = lax.all_to_all(
        grad_hidden.reshape(-1, 2, 4, part), "x", split_axis=2, concat_axis=0, tiled=True
    )
    own_tokens, cotangent, weights = lax.optimization_barrier((own_tokens, cotangent, weights))
    other_tokens = swap_cores(own_tokens)
    cotangent = cotangent.reshape(-1, 2 * part).T.astype(jnp.float32)

    partial = {}
    for offsets in ((7, 0), (6, 1, 5, 2, 4, 3)):
        partial.update(zip(offsets, forward_tiles(offsets, core, own_tokens, other_tokens, weights)))
    right, left = partial[7], partial[0]
    for step in range(4):
        right = ring_shift(right, 1)
        if step < 3:
            left = ring_shift(left, -1)
            right = add_tiles(right, partial[6 - step])
            if step < 2:
                left = add_tiles(left, partial[step + 1])
    total = partial[BEFORE].astype(jnp.float32) + left.astype(jnp.float32) + right.astype(jnp.float32)
    gate_pre = jnp.concatenate([total[:part], total[2 * part : 3 * part]], 0)
    up_pre = jnp.concatenate([total[part : 2 * part], total[3 * part :]], 0)

    sigmoid = jax.nn.sigmoid(gate_pre)
    silu = gate_pre * sigmoid
    hidden = (silu * up_pre).astype(jnp.bfloat16)
    grad_gate = (cotangent * up_pre * sigmoid * (1.0 + gate_pre * (1.0 - sigmoid))).astype(jnp.bfloat16)
    grad_up = (cotangent * silu).astype(jnp.bfloat16)
    grads = jnp.concatenate([grad_gate[:part], grad_up[:part], grad_gate[part:], grad_up[part:]], 0)

    tiles = {BEFORE: grads}
    right = left = grads
    for step in range(1, 5):
        left = ring_shift(left, -1)
        tiles[BEFORE + step] = left
        if step < 4:
            right = ring_shift(right, 1)
            tiles[BEFORE - step] = right
    tiles = [tiles[offset] for offset in range(ROWS)]

    keep, send = token_terms(core, weights, tiles)
    terms = keep + swap_cores(send).astype(jnp.float32)
    terms = lax.all_to_all(
        terms.astype(jnp.bfloat16).reshape(16, -1, features), ("y", "x"), split_axis=0, concat_axis=0, tiled=True
    )
    grad_tokens = jnp.sum(terms.astype(jnp.float32), 0).astype(jnp.bfloat16)
    grad_tokens = lax.ppermute(grad_tokens, ("r", "y", "c", "h"), result_pairs())

    keep, send = weight_grads(core, half, own_tokens, other_tokens, tiles)
    send, hidden = lax.optimization_barrier((send, hidden))
    hidden = lax.all_to_all(
        hidden.T.reshape(-1, 2, 1, part), "x", split_axis=0, concat_axis=2, tiled=True
    ).reshape(-1, hidden_cols)
    grad_weights = keep + lax.ppermute(send, "h", [(0, 1), (1, 0)]).astype(jnp.float32)
    return hidden, grad_tokens, grad_weights[:part].T, grad_weights[part:].T


def solution(mesh):
    fine = Mesh(mesh.devices.reshape(8, 4, 2, 2, 4), ("r", "y", "c", "h", "x"))
    return jax.shard_map(
        local,
        mesh=fine,
        in_specs=(
            P(("r", "h", "x"), ("y", "c")),
            P("r", ("y", "c")),
            P("r", ("y", "c")),
            P(("r", "h", "x"), ("y", "c")),
        ),
        out_specs=(
            P(("r", "h", "x"), ("y", "c")),
            P(("y", "c", "h", "x"), "r"),
            P("r", ("y", "c", "h", "x")),
            P("r", ("y", "c", "h", "x")),
        ),
        check_vma=False,
    )
```

```python
import functools

import jax
import jax.numpy as jnp
from jax import lax
from jax.experimental import pallas as pl
from jax.experimental.pallas import tpu as pltpu
from jax.sharding import Mesh, PartitionSpec as P

RING = 16
ROWS = 8
BEFORE = 3


def ring_index(z):
    z %= RING
    return (z % ROWS) * 2 + z // ROWS


def ring_shift(value, step):
    pairs = [(ring_index(z), ring_index(z + step)) for z in range(RING)]
    return lax.ppermute(value, ("r", "h"), pairs)


def place(z, col):
    z %= RING
    return ((z % ROWS) * ROWS + col) * 2 + z // ROWS


def slot(offset):
    return (offset % 4) * 2 + offset // 4


def token_pairs():
    pairs = []
    for z in range(RING):
        for offset in range(ROWS):
            pairs.append((place(z + offset - BEFORE, z % ROWS), place(z, slot(offset))))
    return pairs


def result_pairs():
    pairs = []
    for z in range(RING):
        for offset in range(ROWS):
            tile = (z + offset - BEFORE) % RING
            pairs.append((place(z, slot(offset)), place(z % ROWS + ROWS * (tile // ROWS), tile % ROWS)))
    return pairs


def dot_f32(left, right, dims=((1,), (0,))):
    return lax.dot_general(left, right, (dims, ((), ())), preferred_element_type=jnp.float32)


SMEM_SPEC = pl.BlockSpec(memory_space=pltpu.SMEM)
VMEM_SPEC = pl.BlockSpec(memory_space=pltpu.VMEM)
PARAMS = pltpu.CompilerParams(vmem_limit_bytes=32 << 20)


def swap_cores(value):
    return lax.ppermute(value, "c", [(0, 1), (1, 0)])


def join_cores(core, own_ref, other_ref, both_ref):
    rows = own_ref.shape[0]
    both_ref[pl.ds(pl.multiple_of(core * rows, rows), rows), :] = own_ref[...]
    both_ref[pl.ds(pl.multiple_of((1 - core) * rows, rows), rows), :] = other_ref[...]


def forward_kernel(offsets, core_ref, own_ref, other_ref, weights_ref, *refs):
    tokens_ref = refs[-1]
    join_cores(core_ref[0], own_ref, other_ref, tokens_ref)
    for offset, tile_ref in zip(offsets, refs):
        product = dot_f32(tokens_ref[offset * 128 : (offset + 1) * 128, :], weights_ref[...])
        tile_ref[...] = product.T.astype(jnp.bfloat16)


def forward_tiles(offsets, core, own, other, weights):
    features, cols = weights.shape
    return pl.pallas_call(
        functools.partial(forward_kernel, offsets),
        in_specs=[SMEM_SPEC] + [VMEM_SPEC] * 3,
        out_specs=[VMEM_SPEC] * len(offsets),
        out_shape=[jax.ShapeDtypeStruct((cols, 128), jnp.bfloat16)] * len(offsets),
        scratch_shapes=[pltpu.VMEM((ROWS * 128, features), jnp.bfloat16)],
        compiler_params=PARAMS,
    )(core, own, other, weights)


def near_kernel(core_ref, own_ref, other_ref, weights_ref, *refs):
    tile_refs = refs[:5]
    terms_ref, sums_ref, tokens_ref, wide_ref = refs[5:]
    join_cores(core_ref[0], own_ref, other_ref, tokens_ref)
    for at, tile_ref in enumerate(tile_refs):
        wide_ref[:, at * 128 : (at + 1) * 128] = tile_ref[...]
        product = dot_f32(weights_ref[...], tile_ref[...])
        terms_ref[at * 128 : (at + 1) * 128, :] = product.T.astype(jnp.bfloat16)
    sums_ref[...] = dot_f32(wide_ref[...], tokens_ref[128:768, :])


def near_products(core, own, other, weights, tiles):
    features, cols = weights.shape
    return pl.pallas_call(
        near_kernel,
        in_specs=[SMEM_SPEC] + [VMEM_SPEC] * 8,
        out_specs=[VMEM_SPEC] * 2,
        out_shape=[
            jax.ShapeDtypeStruct((5 * 128, features), jnp.bfloat16),
            jax.ShapeDtypeStruct((cols, features), jnp.float32),
        ],
        scratch_shapes=[
            pltpu.VMEM((ROWS * 128, features), jnp.bfloat16),
            pltpu.VMEM((cols, 5 * 128), jnp.bfloat16),
        ],
        compiler_params=PARAMS,
    )(core, own, other, weights, *tiles)


def last_kernel(core_ref, half_ref, own_ref, other_ref, weights_ref, terms_ref, sums_ref, *refs):
    tile_refs = refs[:3]
    keep_terms_ref, send_terms_ref, keep_ref, send_ref = refs[3:7]
    tokens_ref, wide_ref, all_terms_ref, all_sums_ref = refs[7:]
    core = core_ref[0]
    half = half_ref[0]
    join_cores(core, own_ref, other_ref, tokens_ref)
    all_terms_ref[128:768, :] = terms_ref[...]
    for at, (offset, tile_ref) in enumerate(zip((0, 6, 7), tile_refs)):
        wide_ref[:, at * 128 : (at + 1) * 128] = tile_ref[...]
        product = dot_f32(weights_ref[...], tile_ref[...])
        all_terms_ref[offset * 128 : (offset + 1) * 128, :] = product.T.astype(jnp.bfloat16)
    tokens_ref[640:768, :] = tokens_ref[0:128, :]
    all_sums_ref[...] = sums_ref[...] + dot_f32(wide_ref[...], tokens_ref[640:1024, :])
    rows = keep_terms_ref.shape[0]
    keep_terms_ref[...] = all_terms_ref[pl.ds(pl.multiple_of(core * rows, rows), rows), :]
    send_terms_ref[...] = all_terms_ref[pl.ds(pl.multiple_of((1 - core) * rows, rows), rows), :]
    rows = keep_ref.shape[0]
    keep_ref[...] = all_sums_ref[pl.ds(pl.multiple_of(half * rows, 16), rows), :]
    send = all_sums_ref[pl.ds(pl.multiple_of((1 - half) * rows, 16), rows), :]
    send_ref[...] = send.astype(jnp.bfloat16)


def last_products(core, half, own, other, weights, terms, sums, tiles):
    features, cols = weights.shape
    return pl.pallas_call(
        last_kernel,
        in_specs=[SMEM_SPEC] * 2 + [VMEM_SPEC] * 8,
        out_specs=[VMEM_SPEC] * 4,
        out_shape=[
            jax.ShapeDtypeStruct((ROWS * 64, features), jnp.bfloat16),
            jax.ShapeDtypeStruct((ROWS * 64, features), jnp.bfloat16),
            jax.ShapeDtypeStruct((cols // 2, features), jnp.float32),
            jax.ShapeDtypeStruct((cols // 2, features), jnp.bfloat16),
        ],
        scratch_shapes=[
            pltpu.VMEM((ROWS * 128, features), jnp.bfloat16),
            pltpu.VMEM((cols, 3 * 128), jnp.bfloat16),
            pltpu.VMEM((ROWS * 128, features), jnp.bfloat16),
            pltpu.VMEM((cols, features), jnp.float32),
        ],
        compiler_params=PARAMS,
    )(core, half, own, other, weights, terms, sums, *tiles)


def add_tiles(*tiles):
    return sum(tile.astype(jnp.float32) for tile in tiles).astype(jnp.bfloat16)


def local(tokens, gate_weight, up_weight, grad_hidden):
    own_x = lax.axis_index("x")
    core = lax.axis_index("c").astype(jnp.int32).reshape(1)
    half = lax.axis_index("h").astype(jnp.int32).reshape(1)
    features, hidden_cols = gate_weight.shape
    part = hidden_cols // 8

    def own_columns(weight, which):
        return lax.dynamic_slice(weight, (0, (which * 4 + own_x) * part), (features, part))

    weights = jnp.concatenate(
        [own_columns(weight, which) for which in (0, 1) for weight in (gate_weight, up_weight)], 1
    )

    piece = lax.ppermute(tokens, ("r", "y", "c", "h"), token_pairs())
    copies = jnp.broadcast_to(piece[None], (16,) + piece.shape)
    own_tokens = lax.all_to_all(copies, ("y", "x"), split_axis=0, concat_axis=0, tiled=True)
    own_tokens = own_tokens.reshape(-1, features)
    cotangent = grad_hidden.reshape(-1, 2, 4, part).transpose(2, 0, 1, 3)
    own_tokens, cotangent, weights = lax.optimization_barrier((own_tokens, cotangent, weights))
    other_tokens = swap_cores(own_tokens)
    cotangent = lax.all_to_all(cotangent, "x", split_axis=0, concat_axis=0, tiled=True)
    cotangent = cotangent.reshape(-1, 2 * part).T.astype(jnp.float32)

    partial = {}
    for offsets in ((6, 7, 0), (5, 1, 4, 2, 3)):
        partial.update(zip(offsets, forward_tiles(offsets, core, own_tokens, other_tokens, weights)))
    right = ring_shift(partial[6], 1)
    left = ring_shift(partial[0], -1)
    right = add_tiles(right, ring_shift(partial[7], 2), partial[5])
    left = add_tiles(left, partial[1])
    right = add_tiles(ring_shift(right, 1), partial[4])
    left = add_tiles(ring_shift(left, -1), partial[2])
    right = ring_shift(right, 1)
    left = ring_shift(left, -1)
    total = partial[BEFORE].astype(jnp.float32) + left.astype(jnp.float32) + right.astype(jnp.float32)
    gate_pre = jnp.concatenate([total[:part], total[2 * part : 3 * part]], 0)
    up_pre = jnp.concatenate([total[part : 2 * part], total[3 * part :]], 0)

    sigmoid = jax.nn.sigmoid(gate_pre)
    silu = gate_pre * sigmoid
    hidden = (silu * up_pre).astype(jnp.bfloat16)
    grad_gate = (cotangent * up_pre * sigmoid * (1.0 + gate_pre * (1.0 - sigmoid))).astype(jnp.bfloat16)
    grad_up = (cotangent * silu).astype(jnp.bfloat16)
    grads = jnp.concatenate([grad_gate[:part], grad_up[:part], grad_gate[part:], grad_up[part:]], 0)

    left_1 = ring_shift(grads, -1)
    right_1 = ring_shift(grads, 1)
    left_2 = ring_shift(left_1, -1)
    right_2 = ring_shift(right_1, 1)
    left_3 = ring_shift(left_2, -1)
    right_3 = ring_shift(right_2, 1)
    left_4 = ring_shift(left_2, -2)
    terms, sums = near_products(
        core, own_tokens, other_tokens, weights, [right_2, right_1, grads, left_1, left_2]
    )
    keep_terms, send_terms, keep, send = last_products(
        core, half, own_tokens, other_tokens, weights, terms, sums, [right_3, left_3, left_4]
    )

    terms = add_tiles(keep_terms, swap_cores(send_terms))
    received = lax.ppermute(send, "h", [(0, 1), (1, 0)])
    terms = lax.all_to_all(
        terms.reshape(16, -1, features), ("y", "x"), split_axis=0, concat_axis=0, tiled=True
    )
    grad_tokens = jnp.sum(terms.astype(jnp.float32), 0).astype(jnp.bfloat16)
    grad_tokens, hidden = lax.optimization_barrier((grad_tokens, hidden))
    grad_tokens = lax.ppermute(grad_tokens, ("r", "y", "c", "h"), result_pairs())
    hidden = lax.all_to_all(
        hidden.T.reshape(-1, 2, 1, part), "x", split_axis=0, concat_axis=2, tiled=True
    ).reshape(-1, hidden_cols)
    grad_tokens, hidden, keep = lax.optimization_barrier((grad_tokens, hidden, keep))
    grad_weights = keep + received.astype(jnp.float32)
    return hidden, grad_tokens, grad_weights[:part].T, grad_weights[part:].T


def solution(mesh):
    fine = Mesh(mesh.devices.reshape(8, 4, 2, 2, 4), ("r", "y", "c", "h", "x"))
    return jax.shard_map(
        local,
        mesh=fine,
        in_specs=(
            P(("r", "h", "x"), ("y", "c")),
            P("r", ("y", "c")),
            P("r", ("y", "c")),
            P(("r", "h", "x"), ("y", "c")),
        ),
        out_specs=(
            P(("r", "h", "x"), ("y", "c")),
            P(("y", "c", "h", "x"), "r"),
            P("r", ("y", "c", "h", "x")),
            P("r", ("y", "c", "h", "x")),
        ),
        check_vma=False,
    )
```

```python
import functools

import jax
import jax.numpy as jnp
from jax import lax
from jax.experimental import pallas as pl
from jax.experimental.pallas import tpu as pltpu
from jax.sharding import Mesh, PartitionSpec as P

RING = 16
ROWS = 8
BEFORE = 3


def ring_index(z):
    z %= RING
    return (z % ROWS) * 2 + z // ROWS


def ring_shift(value, step):
    pairs = [(ring_index(z), ring_index(z + step)) for z in range(RING)]
    return lax.ppermute(value, ("r", "h"), pairs)


def place(z, col):
    z %= RING
    return ((z % ROWS) * ROWS + col) * 2 + z // ROWS


def slot(offset):
    return (offset % 4) * 2 + offset // 4


def token_pairs():
    pairs = []
    for z in range(RING):
        for offset in range(ROWS):
            pairs.append((place(z + offset - BEFORE, z % ROWS), place(z, slot(offset))))
    return pairs


def result_pairs():
    pairs = []
    for z in range(RING):
        for offset in range(ROWS):
            tile = (z + offset - BEFORE) % RING
            pairs.append((place(z, slot(offset)), place(z % ROWS + ROWS * (tile // ROWS), tile % ROWS)))
    return pairs


def dot_f32(left, right, dims=((1,), (0,))):
    return lax.dot_general(left, right, (dims, ((), ())), preferred_element_type=jnp.float32)


SMEM_SPEC = pl.BlockSpec(memory_space=pltpu.SMEM)
VMEM_SPEC = pl.BlockSpec(memory_space=pltpu.VMEM)
PARAMS = pltpu.CompilerParams(vmem_limit_bytes=32 << 20)


def swap_cores(value):
    return lax.ppermute(value, "c", [(0, 1), (1, 0)])


def join_cores(core, own_ref, other_ref, both_ref):
    rows = own_ref.shape[0]
    both_ref[pl.ds(pl.multiple_of(core * rows, rows), rows), :] = own_ref[...]
    both_ref[pl.ds(pl.multiple_of((1 - core) * rows, rows), rows), :] = other_ref[...]


def forward_kernel(offsets, core_ref, own_ref, other_ref, weights_ref, *refs):
    tokens_ref = refs[-1]
    join_cores(core_ref[0], own_ref, other_ref, tokens_ref)
    for offset, tile_ref in zip(offsets, refs):
        product = dot_f32(tokens_ref[offset * 128 : (offset + 1) * 128, :], weights_ref[...])
        tile_ref[...] = product.T.astype(jnp.bfloat16)


def forward_tiles(offsets, core, own, other, weights):
    features, cols = weights.shape
    return pl.pallas_call(
        functools.partial(forward_kernel, offsets),
        in_specs=[SMEM_SPEC] + [VMEM_SPEC] * 3,
        out_specs=[VMEM_SPEC] * len(offsets),
        out_shape=[jax.ShapeDtypeStruct((cols, 128), jnp.bfloat16)] * len(offsets),
        scratch_shapes=[pltpu.VMEM((ROWS * 128, features), jnp.bfloat16)],
        compiler_params=PARAMS,
    )(core, own, other, weights)


def near_kernel(core_ref, own_ref, other_ref, weights_ref, *refs):
    tile_refs = refs[:7]
    terms_ref, sums_ref, tokens_ref, wide_ref = refs[7:]
    join_cores(core_ref[0], own_ref, other_ref, tokens_ref)
    for at, tile_ref in enumerate(tile_refs):
        wide_ref[:, at * 128 : (at + 1) * 128] = tile_ref[...]
        product = dot_f32(weights_ref[...], tile_ref[...])
        terms_ref[at * 128 : (at + 1) * 128, :] = product.T.astype(jnp.bfloat16)
    sums_ref[...] = dot_f32(wide_ref[...], tokens_ref[0:896, :])


def near_products(core, own, other, weights, tiles):
    features, cols = weights.shape
    return pl.pallas_call(
        near_kernel,
        in_specs=[SMEM_SPEC] + [VMEM_SPEC] * 10,
        out_specs=[VMEM_SPEC] * 2,
        out_shape=[
            jax.ShapeDtypeStruct((7 * 128, features), jnp.bfloat16),
            jax.ShapeDtypeStruct((cols, features), jnp.float32),
        ],
        scratch_shapes=[
            pltpu.VMEM((ROWS * 128, features), jnp.bfloat16),
            pltpu.VMEM((cols, 7 * 128), jnp.bfloat16),
        ],
        compiler_params=PARAMS,
    )(core, own, other, weights, *tiles)


def last_sums_kernel(core_ref, half_ref, own_ref, other_ref, sums_ref, tile_ref, keep_ref, send_ref, last_ref):
    rows = own_ref.shape[0]

    @pl.when(core_ref[0] == 0)
    def _():
        last_ref[...] = other_ref[rows - 128 :, :]

    @pl.when(core_ref[0] == 1)
    def _():
        last_ref[...] = own_ref[rows - 128 :, :]

    rows = keep_ref.shape[0]
    half = half_ref[0]
    send_rows = pl.ds(pl.multiple_of((1 - half) * rows, 16), rows)
    keep_rows = pl.ds(pl.multiple_of(half * rows, 16), rows)
    send = sums_ref[send_rows, :] + dot_f32(tile_ref[send_rows, :], last_ref[...])
    send_ref[...] = send.astype(jnp.bfloat16)
    keep_ref[...] = sums_ref[keep_rows, :] + dot_f32(tile_ref[keep_rows, :], last_ref[...])


def last_sums(core, half, own, other, sums, tile):
    cols, features = sums.shape
    return pl.pallas_call(
        last_sums_kernel,
        in_specs=[SMEM_SPEC] * 2 + [VMEM_SPEC] * 4,
        out_specs=[VMEM_SPEC] * 2,
        out_shape=[
            jax.ShapeDtypeStruct((cols // 2, features), jnp.float32),
            jax.ShapeDtypeStruct((cols // 2, features), jnp.bfloat16),
        ],
        scratch_shapes=[pltpu.VMEM((128, features), jnp.bfloat16)],
        compiler_params=PARAMS,
    )(core, half, own, other, sums, tile)


def last_terms_kernel(core_ref, weights_ref, terms_ref, tile_ref, keep_ref, send_ref, all_ref):
    all_ref[0:896, :] = terms_ref[...]
    all_ref[896:1024, :] = dot_f32(weights_ref[...], tile_ref[...]).T.astype(jnp.bfloat16)
    core = core_ref[0]
    rows = keep_ref.shape[0]
    keep_ref[...] = all_ref[pl.ds(pl.multiple_of(core * rows, rows), rows), :]
    send_ref[...] = all_ref[pl.ds(pl.multiple_of((1 - core) * rows, rows), rows), :]


def last_terms(core, weights, terms, tile):
    shape = (ROWS * 64, weights.shape[0])
    return pl.pallas_call(
        last_terms_kernel,
        in_specs=[SMEM_SPEC] + [VMEM_SPEC] * 3,
        out_specs=[VMEM_SPEC] * 2,
        out_shape=[jax.ShapeDtypeStruct(shape, jnp.bfloat16)] * 2,
        scratch_shapes=[pltpu.VMEM((ROWS * 128, shape[1]), jnp.bfloat16)],
        compiler_params=PARAMS,
    )(core, weights, terms, tile)


def add_tiles(*tiles):
    return sum(tile.astype(jnp.float32) for tile in tiles).astype(jnp.bfloat16)


def local(tokens, gate_weight, up_weight, grad_hidden):
    own_x = lax.axis_index("x")
    core = lax.axis_index("c").astype(jnp.int32).reshape(1)
    half = lax.axis_index("h").astype(jnp.int32).reshape(1)
    features, hidden_cols = gate_weight.shape
    part = hidden_cols // 8

    def own_columns(weight, which):
        return lax.dynamic_slice(weight, (0, (which * 4 + own_x) * part), (features, part))

    weights = jnp.concatenate(
        [own_columns(weight, which) for which in (0, 1) for weight in (gate_weight, up_weight)], 1
    )

    piece = lax.ppermute(tokens, ("r", "y", "c", "h"), token_pairs())
    copies = jnp.broadcast_to(piece[None], (16,) + piece.shape)
    own_tokens = lax.all_to_all(copies, ("y", "x"), split_axis=0, concat_axis=0, tiled=True)
    own_tokens = own_tokens.reshape(-1, features)
    cotangent = grad_hidden.reshape(-1, 2, 4, part).transpose(2, 0, 1, 3)
    own_tokens, cotangent, weights = lax.optimization_barrier((own_tokens, cotangent, weights))
    other_tokens = swap_cores(own_tokens)
    cotangent = lax.all_to_all(cotangent, "x", split_axis=0, concat_axis=0, tiled=True)
    partial = {}
    for offsets in ((7, 0), (6, 1, 5, 2, 4, 3)):
        partial.update(zip(offsets, forward_tiles(offsets, core, own_tokens, other_tokens, weights)))
    right = ring_shift(partial[7], 1)
    left = ring_shift(partial[0], -1)
    right, left, cotangent = lax.optimization_barrier((right, left, cotangent))
    right = add_tiles(right, partial[6])
    left = add_tiles(left, partial[1])
    right = add_tiles(ring_shift(right, 1), partial[5])
    left = add_tiles(ring_shift(left, -1), partial[2])
    right = add_tiles(ring_shift(right, 1), partial[4])
    left = ring_shift(left, -1)
    right = ring_shift(right, 1)
    cotangent = cotangent.reshape(-1, 2 * part).T.astype(jnp.float32)
    total = partial[BEFORE].astype(jnp.float32) + left.astype(jnp.float32) + right.astype(jnp.float32)
    gate_pre = jnp.concatenate([total[:part], total[2 * part : 3 * part]], 0)
    up_pre = jnp.concatenate([total[part : 2 * part], total[3 * part :]], 0)

    sigmoid = jax.nn.sigmoid(gate_pre)
    silu = gate_pre * sigmoid
    hidden = (silu * up_pre).astype(jnp.bfloat16)
    grad_gate = (cotangent * up_pre * sigmoid * (1.0 + gate_pre * (1.0 - sigmoid))).astype(jnp.bfloat16)
    grad_up = (cotangent * silu).astype(jnp.bfloat16)
    grads = jnp.concatenate([grad_gate[:part], grad_up[:part], grad_gate[part:], grad_up[part:]], 0)

    left_1 = ring_shift(grads, -1)
    right_1 = ring_shift(grads, 1)
    left_2 = ring_shift(left_1, -1)
    right_2 = ring_shift(right_1, 1)
    left_3 = ring_shift(left_2, -1)
    right_3 = ring_shift(right_2, 1)
    left_4 = ring_shift(left_3, -1)
    terms, sums = near_products(
        core, own_tokens, other_tokens, weights, [right_3, right_2, right_1, grads, left_1, left_2, left_3]
    )
    keep, send = last_sums(core, half, own_tokens, other_tokens, sums, left_4)
    terms, send = lax.optimization_barrier((terms, send))
    keep_terms, send_terms = last_terms(core, weights, terms, left_4)

    terms = add_tiles(keep_terms, swap_cores(send_terms))
    received = lax.ppermute(send, "h", [(0, 1), (1, 0)])
    terms = lax.all_to_all(
        terms.reshape(16, -1, features), ("y", "x"), split_axis=0, concat_axis=0, tiled=True
    )
    grad_tokens = jnp.sum(terms.astype(jnp.float32), 0).astype(jnp.bfloat16)
    grad_tokens, hidden = lax.optimization_barrier((grad_tokens, hidden))
    grad_tokens = lax.ppermute(grad_tokens, ("r", "y", "c", "h"), result_pairs())
    hidden = lax.all_to_all(
        hidden.T.reshape(-1, 2, 1, part), "x", split_axis=0, concat_axis=2, tiled=True
    ).reshape(-1, hidden_cols)
    grad_tokens, hidden, keep = lax.optimization_barrier((grad_tokens, hidden, keep))
    grad_weights = keep + received.astype(jnp.float32)
    return hidden, grad_tokens, grad_weights[:part].T, grad_weights[part:].T


def solution(mesh):
    fine = Mesh(mesh.devices.reshape(8, 4, 2, 2, 4), ("r", "y", "c", "h", "x"))
    return jax.shard_map(
        local,
        mesh=fine,
        in_specs=(
            P(("r", "h", "x"), ("y", "c")),
            P("r", ("y", "c")),
            P("r", ("y", "c")),
            P(("r", "h", "x"), ("y", "c")),
        ),
        out_specs=(
            P(("r", "h", "x"), ("y", "c")),
            P(("y", "c", "h", "x"), "r"),
            P("r", ("y", "c", "h", "x")),
            P("r", ("y", "c", "h", "x")),
        ),
        check_vma=False,
    )
```

```python
import functools

import jax
import jax.numpy as jnp
from jax import lax
from jax.experimental import pallas as pl
from jax.experimental.pallas import tpu as pltpu
from jax.sharding import Mesh, PartitionSpec as P

RING = 16
ROWS = 8
BEFORE = 3


def ring_index(z):
    z %= RING
    return (z % ROWS) * 2 + z // ROWS


def ring_shift(value, step):
    pairs = [(ring_index(z), ring_index(z + step)) for z in range(RING)]
    return lax.ppermute(value, ("r", "h"), pairs)


def place(z, col):
    z %= RING
    return ((z % ROWS) * ROWS + col) * 2 + z // ROWS


def slot(offset):
    return (offset % 4) * 2 + offset // 4


def token_pairs():
    pairs = []
    for z in range(RING):
        for offset in range(ROWS):
            pairs.append((place(z + offset - BEFORE, z % ROWS), place(z, slot(offset))))
    return pairs


def result_pairs():
    pairs = []
    for z in range(RING):
        for offset in range(ROWS):
            tile = (z + offset - BEFORE) % RING
            pairs.append((place(z, slot(offset)), place(z % ROWS + ROWS * (tile // ROWS), tile % ROWS)))
    return pairs


def dot_f32(left, right, dims=((1,), (0,))):
    return lax.dot_general(left, right, (dims, ((), ())), preferred_element_type=jnp.float32)


SMEM_SPEC = pl.BlockSpec(memory_space=pltpu.SMEM)
VMEM_SPEC = pl.BlockSpec(memory_space=pltpu.VMEM)
PARAMS = pltpu.CompilerParams(vmem_limit_bytes=16 << 20)


def swap_cores(value):
    return lax.ppermute(value, "c", [(0, 1), (1, 0)])


def join_cores(core, own_ref, other_ref, both_ref):
    rows = own_ref.shape[0]
    both_ref[pl.ds(pl.multiple_of(core * rows, rows), rows), :] = own_ref[...]
    both_ref[pl.ds(pl.multiple_of((1 - core) * rows, rows), rows), :] = other_ref[...]


def forward_kernel(offsets, core_ref, own_ref, other_ref, weights_ref, *refs):
    tokens_ref = refs[-1]
    join_cores(core_ref[0], own_ref, other_ref, tokens_ref)
    for offset, tile_ref in zip(offsets, refs):
        product = dot_f32(tokens_ref[offset * 128 : (offset + 1) * 128, :], weights_ref[...])
        tile_ref[...] = product.T.astype(jnp.bfloat16)


def forward_tiles(offsets, core, own, other, weights):
    features, cols = weights.shape
    return pl.pallas_call(
        functools.partial(forward_kernel, offsets),
        in_specs=[SMEM_SPEC] + [VMEM_SPEC] * 3,
        out_specs=[VMEM_SPEC] * len(offsets),
        out_shape=[jax.ShapeDtypeStruct((cols, 128), jnp.bfloat16)] * len(offsets),
        scratch_shapes=[pltpu.VMEM((ROWS * 128, features), jnp.bfloat16)],
        compiler_params=PARAMS,
    )(core, own, other, weights)


def near_kernel(core_ref, own_ref, other_ref, weights_ref, *refs):
    tile_refs = refs[:7]
    terms_ref, sums_ref, tokens_ref, wide_ref = refs[7:]
    join_cores(core_ref[0], own_ref, other_ref, tokens_ref)
    for at, tile_ref in enumerate(tile_refs):
        wide_ref[:, at * 128 : (at + 1) * 128] = tile_ref[...]
        product = dot_f32(weights_ref[...], tile_ref[...])
        terms_ref[at * 128 : (at + 1) * 128, :] = product.T.astype(jnp.bfloat16)
    sums_ref[...] = dot_f32(wide_ref[...], tokens_ref[0:896, :])


def near_products(core, own, other, weights, tiles):
    features, cols = weights.shape
    return pl.pallas_call(
        near_kernel,
        in_specs=[SMEM_SPEC] + [VMEM_SPEC] * 10,
        out_specs=[VMEM_SPEC] * 2,
        out_shape=[
            jax.ShapeDtypeStruct((7 * 128, features), jnp.bfloat16),
            jax.ShapeDtypeStruct((cols, features), jnp.float32),
        ],
        scratch_shapes=[
            pltpu.VMEM((ROWS * 128, features), jnp.bfloat16),
            pltpu.VMEM((cols, 7 * 128), jnp.bfloat16),
        ],
        compiler_params=PARAMS,
    )(core, own, other, weights, *tiles)


def last_sums_kernel(core_ref, half_ref, own_ref, other_ref, sums_ref, tile_ref, keep_ref, send_ref, last_ref):
    rows = own_ref.shape[0]

    @pl.when(core_ref[0] == 0)
    def _():
        last_ref[...] = other_ref[rows - 128 :, :]

    @pl.when(core_ref[0] == 1)
    def _():
        last_ref[...] = own_ref[rows - 128 :, :]

    rows = keep_ref.shape[0]
    half = half_ref[0]
    send_rows = pl.ds(pl.multiple_of((1 - half) * rows, 16), rows)
    keep_rows = pl.ds(pl.multiple_of(half * rows, 16), rows)
    send = sums_ref[send_rows, :] + dot_f32(tile_ref[send_rows, :], last_ref[...])
    send_ref[...] = send.astype(jnp.bfloat16)
    keep_ref[...] = sums_ref[keep_rows, :] + dot_f32(tile_ref[keep_rows, :], last_ref[...])


def last_sums(core, half, own, other, sums, tile):
    cols, features = sums.shape
    return pl.pallas_call(
        last_sums_kernel,
        in_specs=[SMEM_SPEC] * 2 + [VMEM_SPEC] * 4,
        out_specs=[VMEM_SPEC] * 2,
        out_shape=[
            jax.ShapeDtypeStruct((cols // 2, features), jnp.float32),
            jax.ShapeDtypeStruct((cols // 2, features), jnp.bfloat16),
        ],
        scratch_shapes=[pltpu.VMEM((128, features), jnp.bfloat16)],
        compiler_params=PARAMS,
    )(core, half, own, other, sums, tile)


def last_terms_kernel(core_ref, weights_ref, terms_ref, tile_ref, keep_ref, send_ref, all_ref):
    all_ref[0:896, :] = terms_ref[...]
    all_ref[896:1024, :] = dot_f32(weights_ref[...], tile_ref[...]).T.astype(jnp.bfloat16)
    core = core_ref[0]
    rows = keep_ref.shape[0]
    keep_ref[...] = all_ref[pl.ds(pl.multiple_of(core * rows, rows), rows), :]
    send_ref[...] = all_ref[pl.ds(pl.multiple_of((1 - core) * rows, rows), rows), :]


def last_terms(core, weights, terms, tile):
    shape = (ROWS * 64, weights.shape[0])
    return pl.pallas_call(
        last_terms_kernel,
        in_specs=[SMEM_SPEC] + [VMEM_SPEC] * 3,
        out_specs=[VMEM_SPEC] * 2,
        out_shape=[jax.ShapeDtypeStruct(shape, jnp.bfloat16)] * 2,
        scratch_shapes=[pltpu.VMEM((ROWS * 128, shape[1]), jnp.bfloat16)],
        compiler_params=PARAMS,
    )(core, weights, terms, tile)


def add_tiles(*tiles):
    return sum(tile.astype(jnp.float32) for tile in tiles).astype(jnp.bfloat16)


def local(tokens, gate_weight, up_weight, grad_hidden):
    own_x = lax.axis_index("x")
    core = lax.axis_index("c").astype(jnp.int32).reshape(1)
    half = lax.axis_index("h").astype(jnp.int32).reshape(1)
    features, hidden_cols = gate_weight.shape
    part = hidden_cols // 8

    def own_columns(weight, which):
        return lax.dynamic_slice(weight, (0, (which * 4 + own_x) * part), (features, part))

    weights = jnp.concatenate(
        [own_columns(weight, which) for which in (0, 1) for weight in (gate_weight, up_weight)], 1
    )

    piece = lax.ppermute(tokens, ("r", "y", "c", "h"), token_pairs())
    copies = jnp.broadcast_to(piece[None], (16,) + piece.shape)
    own_tokens = lax.all_to_all(copies, ("y", "x"), split_axis=0, concat_axis=0, tiled=True)
    own_tokens = own_tokens.reshape(-1, features)
    cotangent = grad_hidden.reshape(-1, 2, 4, part).transpose(2, 0, 1, 3)
    own_tokens, cotangent, weights = lax.optimization_barrier((own_tokens, cotangent, weights))
    other_tokens = swap_cores(own_tokens)
    cotangent = lax.all_to_all(cotangent, "x", split_axis=0, concat_axis=0, tiled=True)
    partial = {}
    for offsets in ((7, 0), (6, 1, 5, 2, 4, 3)):
        partial.update(zip(offsets, forward_tiles(offsets, core, own_tokens, other_tokens, weights)))
    right = ring_shift(partial[7], 1)
    left = ring_shift(partial[0], -1)
    right = add_tiles(right, partial[6])
    left = add_tiles(left, partial[1])
    right = add_tiles(ring_shift(right, 1), partial[5])
    left = add_tiles(ring_shift(left, -1), partial[2])
    right = add_tiles(ring_shift(right, 1), partial[4])
    left = ring_shift(left, -1)
    right, cotangent = lax.optimization_barrier((right, cotangent))
    right = ring_shift(right, 1)
    cotangent = cotangent.reshape(-1, 2 * part).T.astype(jnp.float32)
    total = partial[BEFORE].astype(jnp.float32) + left.astype(jnp.float32) + right.astype(jnp.float32)
    gate_pre = jnp.concatenate([total[:part], total[2 * part : 3 * part]], 0)
    up_pre = jnp.concatenate([total[part : 2 * part], total[3 * part :]], 0)

    sigmoid = jax.nn.sigmoid(gate_pre)
    silu = gate_pre * sigmoid
    hidden = (silu * up_pre).astype(jnp.bfloat16)
    grad_gate = (cotangent * up_pre * sigmoid * (1.0 + gate_pre * (1.0 - sigmoid))).astype(jnp.bfloat16)
    grad_up = (cotangent * silu).astype(jnp.bfloat16)
    grads = jnp.concatenate([grad_gate[:part], grad_up[:part], grad_gate[part:], grad_up[part:]], 0)

    left_1 = ring_shift(grads, -1)
    right_1 = ring_shift(grads, 1)
    left_2 = ring_shift(left_1, -1)
    right_2 = ring_shift(right_1, 1)
    left_3 = ring_shift(left_2, -1)
    right_3 = ring_shift(right_2, 1)
    left_4 = ring_shift(left_3, -1)
    terms, sums = near_products(
        core, own_tokens, other_tokens, weights, [right_3, right_2, right_1, grads, left_1, left_2, left_3]
    )
    keep, send = last_sums(core, half, own_tokens, other_tokens, sums, left_4)
    terms, send = lax.optimization_barrier((terms, send))
    received = lax.ppermute(send, "h", [(0, 1), (1, 0)])
    keep_terms, send_terms = last_terms(core, weights, terms, left_4)
    terms = add_tiles(keep_terms, swap_cores(send_terms))
    terms = lax.all_to_all(
        terms.reshape(16, -1, features), ("y", "x"), split_axis=0, concat_axis=0, tiled=True
    )
    grad_tokens = jnp.sum(terms.astype(jnp.float32), 0).astype(jnp.bfloat16)
    grad_tokens, hidden = lax.optimization_barrier((grad_tokens, hidden))
    hidden = lax.all_to_all(
        hidden.T.reshape(-1, 2, 1, part), "x", split_axis=0, concat_axis=2, tiled=True
    )
    grad_tokens = lax.ppermute(grad_tokens, ("r", "y", "c", "h"), result_pairs())
    grad_tokens, hidden, keep = lax.optimization_barrier((grad_tokens, hidden, keep))
    grad_weights = keep + received.astype(jnp.float32)
    return hidden.reshape(-1, hidden_cols), grad_tokens, grad_weights[:part].T, grad_weights[part:].T


def solution(mesh):
    fine = Mesh(mesh.devices.reshape(8, 4, 2, 2, 4), ("r", "y", "c", "h", "x"))
    return jax.shard_map(
        local,
        mesh=fine,
        in_specs=(
            P(("r", "h", "x"), ("y", "c")),
            P("r", ("y", "c")),
            P("r", ("y", "c")),
            P(("r", "h", "x"), ("y", "c")),
        ),
        out_specs=(
            P(("r", "h", "x"), ("y", "c")),
            P(("y", "c", "h", "x"), "r"),
            P("r", ("y", "c", "h", "x")),
            P("r", ("y", "c", "h", "x")),
        ),
        check_vma=False,
    )
```

```python
import functools

import jax
import jax.numpy as jnp
from jax import lax
from jax.experimental import pallas as pl
from jax.experimental.pallas import tpu as pltpu
from jax.sharding import Mesh, PartitionSpec as P

RING = 16
ROWS = 8
BEFORE = 3


def ring_index(z):
    z %= RING
    return (z % ROWS) * 2 + z // ROWS


def ring_shift(value, step):
    pairs = [(ring_index(z), ring_index(z + step)) for z in range(RING)]
    return lax.ppermute(value, ("r", "h"), pairs)


def place(z, col):
    z %= RING
    return ((z % ROWS) * ROWS + col) * 2 + z // ROWS


def slot(offset):
    return (offset % 4) * 2 + offset // 4


def token_pairs(away):
    pairs = []
    for z in range(RING):
        for offset in range(ROWS):
            pairs.append((place(z + offset - BEFORE, z % ROWS), place(z + away, slot(offset))))
    return pairs


def result_pairs():
    pairs = []
    for z in range(RING):
        for offset in range(ROWS):
            tile = (z + offset - BEFORE) % RING
            pairs.append((place(z, slot(offset)), place(z % ROWS + ROWS * (tile // ROWS), tile % ROWS)))
    return pairs


def dot_f32(left, right, dims=((1,), (0,))):
    return lax.dot_general(left, right, (dims, ((), ())), preferred_element_type=jnp.float32)


SMEM_SPEC = pl.BlockSpec(memory_space=pltpu.SMEM)
VMEM_SPEC = pl.BlockSpec(memory_space=pltpu.VMEM)
PARAMS = pltpu.CompilerParams(vmem_limit_bytes=16 << 20)


def swap_cores(value):
    return lax.ppermute(value, "c", [(0, 1), (1, 0)])


def join_cores(core, own_ref, other_ref, both_ref):
    rows = own_ref.shape[0]
    both_ref[pl.ds(pl.multiple_of(core * rows, rows), rows), :] = own_ref[...]
    both_ref[pl.ds(pl.multiple_of((1 - core) * rows, rows), rows), :] = other_ref[...]


def forward_kernel(offsets, core_ref, own_ref, other_ref, weights_ref, tokens_ref, *refs):
    join_cores(core_ref[0], own_ref, other_ref, tokens_ref)
    for offset, tile_ref in zip(offsets, refs):
        product = dot_f32(tokens_ref[offset * 128 : (offset + 1) * 128, :], weights_ref[...])
        tile_ref[...] = product.T.astype(jnp.bfloat16)


def forward_tiles(offsets, core, own, other, weights):
    features, cols = weights.shape
    tokens = jax.ShapeDtypeStruct((ROWS * 128, features), jnp.bfloat16)
    return pl.pallas_call(
        functools.partial(forward_kernel, offsets),
        in_specs=[SMEM_SPEC] + [VMEM_SPEC] * 3,
        out_specs=[VMEM_SPEC] * (1 + len(offsets)),
        out_shape=[tokens] + [jax.ShapeDtypeStruct((cols, 128), jnp.bfloat16)] * len(offsets),
        compiler_params=PARAMS,
    )(core, own, other, weights)


def step_kernel(rows_at, has_terms, has_sums, outs, half_ref, *refs):
    count = len(rows_at)
    refs = list(refs)
    weights_ref = refs.pop(0) if has_terms else None
    sums_ref = refs.pop(0) if has_sums else None
    token_refs, tile_refs = refs[:count], refs[count : 2 * count]
    tokens_ref, wide_ref = refs[-2:]
    out_refs = refs[2 * count : -2]
    rows = wide_ref.shape[0]
    own_rows = pl.ds(pl.multiple_of(half_ref[0] * rows, 16), rows)
    for at, (first, token_ref, tile_ref) in enumerate(zip(rows_at, token_refs, tile_refs)):
        tokens_ref[at * 128 : (at + 1) * 128, :] = token_ref[first : first + 128, :]
        wide_ref[:, at * 128 : (at + 1) * 128] = tile_ref[own_rows, :]
        if has_terms:
            product = dot_f32(weights_ref[...], tile_ref[...])
            out_refs[outs][at * 128 : (at + 1) * 128, :] = product.T.astype(jnp.bfloat16)
    total = dot_f32(wide_ref[...], tokens_ref[...])
    if has_sums:
        total = total + sums_ref[...]
    rows = rows // outs
    for at, out_ref in enumerate(out_refs[:outs]):
        out_ref[...] = total[at * rows : (at + 1) * rows, :]


def step_products(half, parts, weights=None, sums=None, outs=1):
    tokens = [part[0] for part in parts]
    tiles = [part[2] for part in parts]
    features = tokens[0].shape[1]
    rows = tiles[0].shape[0] // 2
    more = [value for value in (weights, sums) if value is not None]
    shapes = [jax.ShapeDtypeStruct((rows // outs, features), jnp.float32)] * outs
    if weights is not None:
        shapes.append(jax.ShapeDtypeStruct((128 * len(parts), features), jnp.bfloat16))
    rows_at = tuple(part[1] for part in parts)
    return pl.pallas_call(
        functools.partial(step_kernel, rows_at, weights is not None, sums is not None, outs),
        in_specs=[SMEM_SPEC] + [VMEM_SPEC] * (len(more) + 2 * len(parts)),
        out_specs=[VMEM_SPEC] * len(shapes),
        out_shape=shapes,
        scratch_shapes=[
            pltpu.VMEM((128 * len(parts), features), jnp.bfloat16),
            pltpu.VMEM((rows, 128 * len(parts)), jnp.bfloat16),
        ],
        compiler_params=PARAMS,
    )(half, *more, *tokens, *tiles)


def last_terms_kernel(offsets, weights_ref, tile_ref, *refs):
    all_ref = refs[-1]
    for term_ref, term_offsets in zip(refs, offsets):
        for at, offset in enumerate(term_offsets):
            all_ref[slot(offset) * 128 : (slot(offset) + 1) * 128, :] = term_ref[at * 128 : (at + 1) * 128, :]
    all_ref[896:1024, :] = dot_f32(weights_ref[...], tile_ref[...]).T.astype(jnp.bfloat16)


def last_terms(weights, tile, terms, offsets):
    return pl.pallas_call(
        functools.partial(last_terms_kernel, offsets),
        in_specs=[VMEM_SPEC] * (2 + len(terms)),
        out_specs=VMEM_SPEC,
        out_shape=jax.ShapeDtypeStruct((ROWS * 128, weights.shape[0]), jnp.bfloat16),
        compiler_params=PARAMS,
    )(weights, tile, *terms)


def gather_plane(piece):
    copies = jnp.broadcast_to(piece[None], (16,) + piece.shape)
    pieces = lax.all_to_all(copies, ("y", "x"), split_axis=0, concat_axis=0, tiled=True)
    return pieces.reshape(16 * piece.shape[0], piece.shape[1])


def add_tiles(*tiles):
    return sum(tile.astype(jnp.float32) for tile in tiles).astype(jnp.bfloat16)


def local(tokens, gate_weight, up_weight, grad_hidden):
    own_x = lax.axis_index("x")
    core = lax.axis_index("c").astype(jnp.int32).reshape(1)
    half = lax.axis_index("h").astype(jnp.int32).reshape(1)
    features, hidden_cols = gate_weight.shape
    part = hidden_cols // 8

    def own_columns(weight, which):
        return lax.dynamic_slice(weight, (0, (which * 4 + own_x) * part), (features, part))

    weights = jnp.concatenate(
        [own_columns(weight, which) for which in (0, 1) for weight in (gate_weight, up_weight)], 1
    )

    piece = lax.ppermute(tokens, ("r", "y", "c", "h"), token_pairs(0))
    far_piece = lax.ppermute(tokens, ("r", "y", "c", "h"), token_pairs(8))
    own_tokens = gather_plane(piece)
    cotangent = grad_hidden.reshape(-1, 2, 4, part).transpose(2, 0, 1, 3)
    own_tokens, far_piece, cotangent, weights = lax.optimization_barrier(
        (own_tokens, far_piece, cotangent, weights)
    )
    other_tokens = swap_cores(own_tokens)
    cotangent = lax.all_to_all(cotangent, "x", split_axis=0, concat_axis=0, tiled=True)
    partial = {}
    for offsets in ((7, 0), (6, 1, 5, 2, 4, 3)):
        near_tokens, *products = forward_tiles(offsets, core, own_tokens, other_tokens, weights)
        partial.update(zip(offsets, products))
    right = ring_shift(partial[7], 1)
    left = ring_shift(partial[0], -1)
    right = add_tiles(right, partial[6])
    left = add_tiles(left, partial[1])
    right = add_tiles(ring_shift(right, 1), partial[5])
    left = add_tiles(ring_shift(left, -1), partial[2])
    right = add_tiles(ring_shift(right, 1), partial[4])
    left = ring_shift(left, -1)
    far_own = gather_plane(far_piece)
    right, cotangent = lax.optimization_barrier((right, cotangent))
    right = ring_shift(right, 1)
    right, left, far_own = lax.optimization_barrier((right, left, far_own))
    far_other = swap_cores(far_own)
    cotangent = cotangent.reshape(-1, 2 * part).T.astype(jnp.float32)
    total = partial[BEFORE].astype(jnp.float32) + left.astype(jnp.float32) + right.astype(jnp.float32)
    gate_pre = jnp.concatenate([total[:part], total[2 * part : 3 * part]], 0)
    up_pre = jnp.concatenate([total[part : 2 * part], total[3 * part :]], 0)

    sigmoid = jax.nn.sigmoid(gate_pre)
    silu = gate_pre * sigmoid
    hidden = (silu * up_pre).astype(jnp.bfloat16)
    grad_gate = (cotangent * up_pre * sigmoid * (1.0 + gate_pre * (1.0 - sigmoid))).astype(jnp.bfloat16)
    grad_up = (cotangent * silu).astype(jnp.bfloat16)
    grads = jnp.concatenate([grad_gate[:part], grad_up[:part], grad_gate[part:], grad_up[part:]], 0)

    far_tokens = jnp.where(
        core[0] == 0, jnp.concatenate([far_own, far_other], 0), jnp.concatenate([far_other, far_own], 0)
    )
    left = right = grads
    parts = [(near_tokens, BEFORE * 128, grads)]
    terms = []
    offsets = ((3, 4, 2), (5, 1), (6, 0))
    sums = None
    for step in range(1, 4):
        left = ring_shift(left, -1)
        right = ring_shift(right, 1)
        parts += [(near_tokens, (BEFORE + step) * 128, left), (near_tokens, (BEFORE - step) * 128, right)]
        sums, step_terms = step_products(half, parts, weights, sums)
        terms.append(step_terms)
        parts = []
    left = ring_shift(left, -1)
    right = ring_shift(right, 1)
    parts = [(near_tokens, 7 * 128, left), (far_tokens, 7 * 128, right)]
    terms = last_terms(weights, left, terms, offsets)
    left, right, terms = lax.optimization_barrier((left, right, terms))
    terms = lax.all_to_all(
        terms.reshape(32, -1, features), ("y", "c", "x"), split_axis=0, concat_axis=0, tiled=True
    )
    for step in range(5, 9):
        left = ring_shift(left, -1)
        parts.append((far_tokens, (step - 5) * 128, left))
        if step < 8:
            right = ring_shift(right, 1)
            parts.append((far_tokens, (11 - step) * 128, right))
        if step < 7:
            (sums,) = step_products(half, parts, sums=sums)
            parts = []
        if step == 6:
            left, right, terms = lax.optimization_barrier((left, right, terms))
            grad_tokens = jnp.sum(terms.astype(jnp.float32), 0).astype(jnp.bfloat16)
            grad_tokens = lax.ppermute(grad_tokens, ("r", "y", "c", "h"), result_pairs())
            left, hidden = lax.optimization_barrier((left, hidden))
            hidden = lax.all_to_all(
                hidden.T.reshape(-1, 2, 1, part), "x", split_axis=0, concat_axis=2, tiled=True
            )
    gate_grad, up_grad = step_products(half, parts, sums=sums, outs=2)
    return hidden.reshape(-1, hidden_cols), grad_tokens, gate_grad.T, up_grad.T


def solution(mesh):
    fine = Mesh(mesh.devices.reshape(8, 4, 2, 2, 4), ("r", "y", "c", "h", "x"))
    return jax.shard_map(
        local,
        mesh=fine,
        in_specs=(
            P(("r", "h", "x"), ("y", "c")),
            P("r", ("y", "c")),
            P("r", ("y", "c")),
            P(("r", "h", "x"), ("y", "c")),
        ),
        out_specs=(
            P(("r", "h", "x"), ("y", "c")),
            P(("y", "c", "h", "x"), "r"),
            P("r", ("y", "c", "h", "x")),
            P("r", ("y", "c", "h", "x")),
        ),
        check_vma=False,
    )
```

```python
import functools

import jax
import jax.numpy as jnp
from jax import lax
from jax.experimental import pallas as pl
from jax.experimental.pallas import tpu as pltpu
from jax.sharding import Mesh, PartitionSpec as P

RING = 16
ROWS = 8
BEFORE = 3


def ring_index(z):
    z %= RING
    return (z % ROWS) * 2 + z // ROWS


def ring_shift(value, step):
    pairs = [(ring_index(z), ring_index(z + step)) for z in range(RING)]
    return lax.ppermute(value, ("r", "h"), pairs)


def place(z, col):
    z %= RING
    return ((z % ROWS) * ROWS + col) * 2 + z // ROWS


def slot(offset):
    return (offset % 4) * 2 + offset // 4


def token_pairs():
    pairs = []
    for z in range(RING):
        for offset in range(ROWS):
            pairs.append((place(z + offset - BEFORE, z % ROWS), place(z, slot(offset))))
    return pairs


def result_pairs():
    pairs = []
    for z in range(RING):
        for offset in range(ROWS):
            tile = (z + offset - BEFORE) % RING
            pairs.append((place(z, slot(offset)), place(z % ROWS + ROWS * (tile // ROWS), tile % ROWS)))
    return pairs


def dot_f32(left, right, dims=((1,), (0,))):
    return lax.dot_general(left, right, (dims, ((), ())), preferred_element_type=jnp.float32)


SMEM_SPEC = pl.BlockSpec(memory_space=pltpu.SMEM)
VMEM_SPEC = pl.BlockSpec(memory_space=pltpu.VMEM)
PARAMS = pltpu.CompilerParams(vmem_limit_bytes=16 << 20)


def swap_cores(value):
    return lax.ppermute(value, "c", [(0, 1), (1, 0)])


def join_cores(core, own_ref, other_ref, both_ref):
    rows = own_ref.shape[0]
    both_ref[pl.ds(pl.multiple_of(core * rows, rows), rows), :] = own_ref[...]
    both_ref[pl.ds(pl.multiple_of((1 - core) * rows, rows), rows), :] = other_ref[...]


def forward_kernel(offsets, core_ref, own_ref, other_ref, weights_ref, *refs):
    tokens_ref = refs[-1]
    join_cores(core_ref[0], own_ref, other_ref, tokens_ref)
    for offset, tile_ref in zip(offsets, refs):
        product = dot_f32(tokens_ref[offset * 128 : (offset + 1) * 128, :], weights_ref[...])
        tile_ref[...] = product.T.astype(jnp.bfloat16)


def forward_tiles(offsets, core, own, other, weights):
    features, cols = weights.shape
    return pl.pallas_call(
        functools.partial(forward_kernel, offsets),
        in_specs=[SMEM_SPEC] + [VMEM_SPEC] * 3,
        out_specs=[VMEM_SPEC] * len(offsets),
        out_shape=[jax.ShapeDtypeStruct((cols, 128), jnp.bfloat16)] * len(offsets),
        scratch_shapes=[pltpu.VMEM((ROWS * 128, features), jnp.bfloat16)],
        compiler_params=PARAMS,
    )(core, own, other, weights)


def near_kernel(core_ref, own_ref, other_ref, weights_ref, *refs):
    tile_refs = refs[:7]
    terms_ref, sums_ref, tokens_ref, wide_ref = refs[7:]
    join_cores(core_ref[0], own_ref, other_ref, tokens_ref)
    for at, tile_ref in enumerate(tile_refs):
        wide_ref[:, at * 128 : (at + 1) * 128] = tile_ref[...]
        product = dot_f32(weights_ref[...], tile_ref[...])
        terms_ref[slot(at) * 128 : (slot(at) + 1) * 128, :] = product.T.astype(jnp.bfloat16)
    sums_ref[...] = dot_f32(wide_ref[...], tokens_ref[0:896, :])


def near_products(core, own, other, weights, tiles):
    features, cols = weights.shape
    return pl.pallas_call(
        near_kernel,
        in_specs=[SMEM_SPEC] + [VMEM_SPEC] * 10,
        out_specs=[VMEM_SPEC] * 2,
        out_shape=[
            jax.ShapeDtypeStruct((7 * 128, features), jnp.bfloat16),
            jax.ShapeDtypeStruct((cols, features), jnp.float32),
        ],
        scratch_shapes=[
            pltpu.VMEM((ROWS * 128, features), jnp.bfloat16),
            pltpu.VMEM((cols, 7 * 128), jnp.bfloat16),
        ],
        compiler_params=PARAMS,
    )(core, own, other, weights, *tiles)


def last_sums_kernel(core_ref, half_ref, own_ref, other_ref, sums_ref, tile_ref, keep_ref, send_ref, last_ref):
    rows = own_ref.shape[0]

    @pl.when(core_ref[0] == 0)
    def _():
        last_ref[...] = other_ref[rows - 128 :, :]

    @pl.when(core_ref[0] == 1)
    def _():
        last_ref[...] = own_ref[rows - 128 :, :]

    rows = keep_ref.shape[0]
    half = half_ref[0]
    send_rows = pl.ds(pl.multiple_of((1 - half) * rows, 16), rows)
    keep_rows = pl.ds(pl.multiple_of(half * rows, 16), rows)
    send = sums_ref[send_rows, :] + dot_f32(tile_ref[send_rows, :], last_ref[...])
    send_ref[...] = send.astype(jnp.bfloat16)
    keep_ref[...] = sums_ref[keep_rows, :] + dot_f32(tile_ref[keep_rows, :], last_ref[...])


def last_sums(core, half, own, other, sums, tile):
    cols, features = sums.shape
    return pl.pallas_call(
        last_sums_kernel,
        in_specs=[SMEM_SPEC] * 2 + [VMEM_SPEC] * 4,
        out_specs=[VMEM_SPEC] * 2,
        out_shape=[
            jax.ShapeDtypeStruct((cols // 2, features), jnp.float32),
            jax.ShapeDtypeStruct((cols // 2, features), jnp.bfloat16),
        ],
        scratch_shapes=[pltpu.VMEM((128, features), jnp.bfloat16)],
        compiler_params=PARAMS,
    )(core, half, own, other, sums, tile)


def last_terms_kernel(weights_ref, terms_ref, tile_ref, all_ref):
    all_ref[0:896, :] = terms_ref[...]
    all_ref[896:1024, :] = dot_f32(weights_ref[...], tile_ref[...]).T.astype(jnp.bfloat16)


def last_terms(weights, terms, tile):
    return pl.pallas_call(
        last_terms_kernel,
        in_specs=[VMEM_SPEC] * 3,
        out_specs=VMEM_SPEC,
        out_shape=jax.ShapeDtypeStruct((ROWS * 128, weights.shape[0]), jnp.bfloat16),
        compiler_params=PARAMS,
    )(weights, terms, tile)


def add_tiles(*tiles):
    return sum(tile.astype(jnp.float32) for tile in tiles).astype(jnp.bfloat16)


def local(tokens, gate_weight, up_weight, grad_hidden):
    own_x = lax.axis_index("x")
    core = lax.axis_index("c").astype(jnp.int32).reshape(1)
    half = lax.axis_index("h").astype(jnp.int32).reshape(1)
    features, hidden_cols = gate_weight.shape
    part = hidden_cols // 8

    def own_columns(weight, which):
        return lax.dynamic_slice(weight, (0, (which * 4 + own_x) * part), (features, part))

    weights = jnp.concatenate(
        [own_columns(weight, which) for which in (0, 1) for weight in (gate_weight, up_weight)], 1
    )

    piece = lax.ppermute(tokens, ("r", "y", "c", "h"), token_pairs())
    copies = jnp.broadcast_to(piece[None], (16,) + piece.shape)
    own_tokens = lax.all_to_all(copies, ("y", "x"), split_axis=0, concat_axis=0, tiled=True)
    own_tokens = own_tokens.reshape(-1, features)
    cotangent = grad_hidden.reshape(-1, 2, 4, part).transpose(2, 0, 1, 3)
    own_tokens, cotangent, weights = lax.optimization_barrier((own_tokens, cotangent, weights))
    other_tokens = swap_cores(own_tokens)
    cotangent = lax.all_to_all(cotangent, "x", split_axis=0, concat_axis=0, tiled=True)
    partial = {}
    for offsets in ((7, 0), (6, 1, 5, 2, 4, 3)):
        partial.update(zip(offsets, forward_tiles(offsets, core, own_tokens, other_tokens, weights)))
    right = ring_shift(partial[7], 1)
    left = ring_shift(partial[0], -1)
    right = add_tiles(right, partial[6])
    left = add_tiles(left, partial[1])
    right = add_tiles(ring_shift(right, 1), partial[5])
    left = add_tiles(ring_shift(left, -1), partial[2])
    right = add_tiles(ring_shift(right, 1), partial[4])
    left = ring_shift(left, -1)
    right, cotangent = lax.optimization_barrier((right, cotangent))
    right = ring_shift(right, 1)
    cotangent = cotangent.reshape(-1, 2 * part).T.astype(jnp.float32)
    total = partial[BEFORE].astype(jnp.float32) + left.astype(jnp.float32) + right.astype(jnp.float32)
    gate_pre = jnp.concatenate([total[:part], total[2 * part : 3 * part]], 0)
    up_pre = jnp.concatenate([total[part : 2 * part], total[3 * part :]], 0)

    sigmoid = jax.nn.sigmoid(gate_pre)
    silu = gate_pre * sigmoid
    hidden = (silu * up_pre).astype(jnp.bfloat16)
    grad_gate = (cotangent * up_pre * sigmoid * (1.0 + gate_pre * (1.0 - sigmoid))).astype(jnp.bfloat16)
    grad_up = (cotangent * silu).astype(jnp.bfloat16)
    grads = jnp.concatenate([grad_gate[:part], grad_up[:part], grad_gate[part:], grad_up[part:]], 0)

    left_1 = ring_shift(grads, -1)
    right_1 = ring_shift(grads, 1)
    left_2 = ring_shift(left_1, -1)
    right_2 = ring_shift(right_1, 1)
    left_3 = ring_shift(left_2, -1)
    right_3 = ring_shift(right_2, 1)
    left_4 = ring_shift(left_3, -1)
    terms, sums = near_products(
        core, own_tokens, other_tokens, weights, [right_3, right_2, right_1, grads, left_1, left_2, left_3]
    )
    keep, send = last_sums(core, half, own_tokens, other_tokens, sums, left_4)
    terms, send = lax.optimization_barrier((terms, send))
    received = lax.ppermute(send, "h", [(0, 1), (1, 0)])
    terms = last_terms(weights, terms, left_4)
    terms = lax.all_to_all(
        terms.reshape(32, -1, features), ("y", "c", "x"), split_axis=0, concat_axis=0, tiled=True
    )
    grad_tokens = jnp.sum(terms.astype(jnp.float32), 0).astype(jnp.bfloat16)
    grad_tokens, hidden = lax.optimization_barrier((grad_tokens, hidden))
    hidden = lax.all_to_all(
        hidden.T.reshape(-1, 2, 1, part), "x", split_axis=0, concat_axis=2, tiled=True
    )
    grad_tokens = lax.ppermute(grad_tokens, ("r", "y", "c", "h"), result_pairs())
    grad_tokens, hidden, keep = lax.optimization_barrier((grad_tokens, hidden, keep))
    grad_weights = keep + received.astype(jnp.float32)
    return hidden.reshape(-1, hidden_cols), grad_tokens, grad_weights[:part].T, grad_weights[part:].T


def solution(mesh):
    fine = Mesh(mesh.devices.reshape(8, 4, 2, 2, 4), ("r", "y", "c", "h", "x"))
    return jax.shard_map(
        local,
        mesh=fine,
        in_specs=(
            P(("r", "h", "x"), ("y", "c")),
            P("r", ("y", "c")),
            P("r", ("y", "c")),
            P(("r", "h", "x"), ("y", "c")),
        ),
        out_specs=(
            P(("r", "h", "x"), ("y", "c")),
            P(("y", "c", "h", "x"), "r"),
            P("r", ("y", "c", "h", "x")),
            P("r", ("y", "c", "h", "x")),
        ),
        check_vma=False,
    )
```

```python
import functools

import jax
import jax.numpy as jnp
from jax import lax
from jax.experimental import pallas as pl
from jax.experimental.pallas import tpu as pltpu
from jax.sharding import Mesh, PartitionSpec as P

RING = 16
ROWS = 8
FORWARD = ((3, -1), (3, 0), (3, 1), (0, -1), (0, 0), (0, 1), (-3, -1), (-3, 0))
BACKWARD = ((-3, 0), (-2, 0), (-1, 0), (0, 0), (1, 0), (2, 0), (3, 0), (3, -1))


def ring_index(z):
    z %= RING
    return (z % ROWS) * 2 + z // ROWS


def ring_shift(value, step):
    pairs = [(ring_index(z), ring_index(z + step)) for z in range(RING)]
    return lax.ppermute(value, ("r", "h"), pairs)


def place(z, col):
    z %= RING
    return ((z % ROWS) * ROWS + col) * 2 + z // ROWS


def slot(at):
    return (at % 4) * 2 + at // 4


def token_pairs():
    pairs = []
    for z in range(RING):
        for at, (ahead, block) in enumerate(FORWARD):
            pairs.append((place(z + ahead, (z + block) % ROWS), place(z, slot(at))))
    return pairs


def result_pairs():
    pairs = []
    for z in range(RING):
        for at, (ahead, block) in enumerate(BACKWARD):
            tile = (z + ahead) % RING
            row = (z + block) % ROWS
            pairs.append((place(z, slot(at)), place(row + ROWS * (tile // ROWS), tile % ROWS)))
    return pairs


def dot_f32(left, right, dims=((1,), (0,))):
    return lax.dot_general(left, right, (dims, ((), ())), preferred_element_type=jnp.float32)


SMEM_SPEC = pl.BlockSpec(memory_space=pltpu.SMEM)
VMEM_SPEC = pl.BlockSpec(memory_space=pltpu.VMEM)
PARAMS = pltpu.CompilerParams(vmem_limit_bytes=16 << 20)


def swap_cores(value):
    return lax.ppermute(value, "c", [(0, 1), (1, 0)])


def join_cores(core, own_ref, other_ref, both_ref):
    rows = own_ref.shape[0]
    both_ref[pl.ds(pl.multiple_of(core * rows, rows), rows), :] = own_ref[...]
    both_ref[pl.ds(pl.multiple_of((1 - core) * rows, rows), rows), :] = other_ref[...]


def tile_product(tokens_ref, ats, weights_refs):
    total = 0.0
    for at, weights_ref in zip(ats, weights_refs):
        total = total + dot_f32(tokens_ref[at * 128 : (at + 1) * 128, :], weights_ref[...])
    return total.T


def sends_kernel(core_ref, own_ref, other_ref, below_ref, here_ref, above_ref, up_ref, down_ref, tokens_ref):
    join_cores(core_ref[0], own_ref, other_ref, tokens_ref)
    weights_refs = (below_ref, here_ref, above_ref)
    up_ref[...] = tile_product(tokens_ref, (0, 1, 2), weights_refs).astype(jnp.bfloat16)
    down_ref[...] = tile_product(tokens_ref, (6, 7), weights_refs).astype(jnp.bfloat16)


def own_kernel(core_ref, own_ref, other_ref, below_ref, here_ref, above_ref, out_ref, *refs):
    tokens_ref = refs[-1]
    join_cores(core_ref[0], own_ref, other_ref, tokens_ref)
    out_ref[...] = tile_product(tokens_ref, (3, 4, 5), (below_ref, here_ref, above_ref))
    for tokens_out_ref, ats in zip(refs, ((0, 3, 6), (2, 5), (7, 4, 1))):
        for row, at in enumerate(ats):
            tokens_out_ref[row * 128 : (row + 1) * 128, :] = tokens_ref[at * 128 : (at + 1) * 128, :]


def forward(kernel, outs, core, own, other, weights):
    return pl.pallas_call(
        kernel,
        in_specs=[SMEM_SPEC] + [VMEM_SPEC] * 5,
        out_specs=[VMEM_SPEC] * len(outs),
        out_shape=outs,
        scratch_shapes=[pltpu.VMEM((ROWS * 128, own.shape[1]), jnp.bfloat16)],
        compiler_params=PARAMS,
    )(core, own, other, *weights)


def forward_sends(core, own, other, weights):
    tile = jax.ShapeDtypeStruct((weights[0].shape[1], 128), jnp.bfloat16)
    return forward(sends_kernel, [tile, tile], core, own, other, weights)


def own_sums(core, own, other, weights):
    features, cols = weights[0].shape
    outs = [jax.ShapeDtypeStruct((cols, 128), jnp.float32)]
    outs += [jax.ShapeDtypeStruct((128 * count, features), jnp.bfloat16) for count in (3, 2, 3)]
    return forward(own_kernel, outs, core, own, other, weights)


def near_kernel(weights_ref, mine_ref, right_ref, left_ref, *refs):
    tile_refs = refs[:5]
    terms_ref, sums_ref, tokens_ref, wide_ref = refs[5:]
    sources = ((right_ref, 2), (left_ref, 1), (mine_ref, 1), (right_ref, 1), (left_ref, 0))
    for at, (tile_ref, (source_ref, row)) in enumerate(zip(tile_refs, sources)):
        tokens_ref[at * 128 : (at + 1) * 128, :] = source_ref[row * 128 : (row + 1) * 128, :]
        wide_ref[:, at * 128 : (at + 1) * 128] = tile_ref[...]
        product = dot_f32(weights_ref[...], tile_ref[...])
        terms_ref[at * 128 : (at + 1) * 128, :] = product.T.astype(jnp.bfloat16)
    sums_ref[...] = dot_f32(wide_ref[...], tokens_ref[...])


def near_products(weights, mine, right, left, tiles):
    features, cols = weights.shape
    return pl.pallas_call(
        near_kernel,
        in_specs=[VMEM_SPEC] * 9,
        out_specs=[VMEM_SPEC] * 2,
        out_shape=[
            jax.ShapeDtypeStruct((5 * 128, features), jnp.bfloat16),
            jax.ShapeDtypeStruct((cols, features), jnp.float32),
        ],
        scratch_shapes=[
            pltpu.VMEM((5 * 128, features), jnp.bfloat16),
            pltpu.VMEM((cols, 5 * 128), jnp.bfloat16),
        ],
        compiler_params=PARAMS,
    )(weights, mine, right, left, *tiles)


def third_kernel(here_ref, below_ref, mine_ref, terms_ref, sums_ref, low_ref, high_ref, *refs):
    all_ref, out_ref, tokens_ref, wide_ref = refs
    for at in range(1, 6):
        all_ref[slot(at) * 128 : (slot(at) + 1) * 128, :] = terms_ref[(at - 1) * 128 : at * 128, :]
    for at, tile_ref, weights_ref in ((0, low_ref, here_ref), (6, high_ref, here_ref), (7, high_ref, below_ref)):
        product = dot_f32(weights_ref[...], tile_ref[...])
        all_ref[slot(at) * 128 : (slot(at) + 1) * 128, :] = product.T.astype(jnp.bfloat16)
    tokens_ref[0:128, :] = mine_ref[0:128, :]
    tokens_ref[128:256, :] = mine_ref[256:384, :]
    wide_ref[:, 0:128] = low_ref[...]
    wide_ref[:, 128:256] = high_ref[...]
    out_ref[...] = sums_ref[...] + dot_f32(wide_ref[...], tokens_ref[...])


def third_products(here, below, mine, terms, sums, low, high):
    features, cols = here.shape
    return pl.pallas_call(
        third_kernel,
        in_specs=[VMEM_SPEC] * 7,
        out_specs=[VMEM_SPEC] * 2,
        out_shape=[
            jax.ShapeDtypeStruct((ROWS * 128, features), jnp.bfloat16),
            jax.ShapeDtypeStruct((cols, features), jnp.float32),
        ],
        scratch_shapes=[
            pltpu.VMEM((256, features), jnp.bfloat16),
            pltpu.VMEM((cols, 256), jnp.bfloat16),
        ],
        compiler_params=PARAMS,
    )(here, below, mine, terms, sums, low, high)


def last_kernel(half_ref, right_ref, sums_ref, tile_ref, keep_ref, send_ref):
    rows = keep_ref.shape[0]
    half = half_ref[0]
    send_rows = pl.ds(pl.multiple_of((1 - half) * rows, 16), rows)
    keep_rows = pl.ds(pl.multiple_of(half * rows, 16), rows)
    tokens = right_ref[0:128, :]
    send = sums_ref[send_rows, :] + dot_f32(tile_ref[send_rows, :], tokens)
    send_ref[...] = send.astype(jnp.bfloat16)
    keep_ref[...] = sums_ref[keep_rows, :] + dot_f32(tile_ref[keep_rows, :], tokens)


def last_sums(half, right, sums, tile):
    cols, features = sums.shape
    shape = (cols // 2, features)
    return pl.pallas_call(
        last_kernel,
        in_specs=[SMEM_SPEC] + [VMEM_SPEC] * 3,
        out_specs=[VMEM_SPEC] * 2,
        out_shape=[jax.ShapeDtypeStruct(shape, jnp.float32), jax.ShapeDtypeStruct(shape, jnp.bfloat16)],
        compiler_params=PARAMS,
    )(half, right, sums, tile)


def local(tokens, gate_weight, up_weight, grad_hidden):
    own_x = lax.axis_index("x")
    core = lax.axis_index("c").astype(jnp.int32).reshape(1)
    half = lax.axis_index("h").astype(jnp.int32).reshape(1)
    features, hidden_cols = gate_weight.shape
    part = hidden_cols // 8

    def own_columns(weight, which):
        return lax.dynamic_slice(weight, (0, (which * 4 + own_x) * part), (features, part))

    weights = jnp.concatenate(
        [own_columns(weight, which) for which in (0, 1) for weight in (gate_weight, up_weight)], 1
    )

    piece = lax.ppermute(tokens, ("r", "y", "c", "h"), token_pairs())
    piece, weights = lax.optimization_barrier((piece, weights))
    below = ring_shift(weights, 1)
    above = ring_shift(weights, -1)
    copies = jnp.broadcast_to(piece[None], (16,) + piece.shape)
    own_tokens = lax.all_to_all(copies, ("y", "x"), split_axis=0, concat_axis=0, tiled=True)
    own_tokens = own_tokens.reshape(-1, features)
    cotangent = grad_hidden.reshape(-1, 2, 4, part).transpose(2, 0, 1, 3)
    own_tokens, cotangent, below, above = lax.optimization_barrier((own_tokens, cotangent, below, above))
    other_tokens = swap_cores(own_tokens)
    cotangent = lax.all_to_all(cotangent, "x", split_axis=0, concat_axis=0, tiled=True)

    rows = (below, weights, above)
    up, down = forward_sends(core, own_tokens, other_tokens, rows)
    from_below = ring_shift(up, 3)
    from_above = ring_shift(down, -3)
    total, to_left, to_right, mine = own_sums(core, own_tokens, other_tokens, rows)
    right_tokens = ring_shift(to_left, -1)
    left_tokens = ring_shift(to_right, 1)
    from_below, from_above, cotangent = lax.optimization_barrier((from_below, from_above, cotangent))
    cotangent = cotangent.reshape(-1, 2 * part).T.astype(jnp.float32)
    total = total + from_below.astype(jnp.float32) + from_above.astype(jnp.float32)
    gate_pre = jnp.concatenate([total[:part], total[2 * part : 3 * part]], 0)
    up_pre = jnp.concatenate([total[part : 2 * part], total[3 * part :]], 0)

    sigmoid = jax.nn.sigmoid(gate_pre)
    silu = gate_pre * sigmoid
    hidden = (silu * up_pre).astype(jnp.bfloat16)
    grad_gate = (cotangent * up_pre * sigmoid * (1.0 + gate_pre * (1.0 - sigmoid))).astype(jnp.bfloat16)
    grad_up = (cotangent * silu).astype(jnp.bfloat16)
    grads = jnp.concatenate([grad_gate[:part], grad_up[:part], grad_gate[part:], grad_up[part:]], 0)

    left_1 = ring_shift(grads, -1)
    right_1 = ring_shift(grads, 1)
    left_2 = ring_shift(left_1, -1)
    right_2 = ring_shift(right_1, 1)
    left_3 = ring_shift(left_2, -1)
    right_3 = ring_shift(right_2, 1)
    terms, sums = near_products(
        weights, mine, right_tokens, left_tokens, [right_2, right_1, grads, left_1, left_2]
    )
    left_3, right_3, terms, sums = lax.optimization_barrier((left_3, right_3, terms, sums))
    left_4 = ring_shift(left_3, -1)
    terms, sums = third_products(weights, below, mine, terms, sums, right_3, left_3)
    left_4, terms = lax.optimization_barrier((left_4, terms))
    terms = lax.all_to_all(
        terms.reshape(32, -1, features), ("y", "c", "x"), split_axis=0, concat_axis=0, tiled=True
    )
    keep, send = last_sums(half, right_tokens, sums, left_4)
    received = lax.ppermute(send, "h", [(0, 1), (1, 0)])
    grad_tokens = jnp.sum(terms.astype(jnp.float32), 0).astype(jnp.bfloat16)
    grad_tokens, hidden = lax.optimization_barrier((grad_tokens, hidden))
    hidden = lax.all_to_all(
        hidden.T.reshape(-1, 2, 1, part), "x", split_axis=0, concat_axis=2, tiled=True
    )
    grad_tokens = lax.ppermute(grad_tokens, ("r", "y", "c", "h"), result_pairs())
    grad_tokens, hidden, keep = lax.optimization_barrier((grad_tokens, hidden, keep))
    grad_weights = keep + received.astype(jnp.float32)
    return hidden.reshape(-1, hidden_cols), grad_tokens, grad_weights[:part].T, grad_weights[part:].T


def solution(mesh):
    fine = Mesh(mesh.devices.reshape(8, 4, 2, 2, 4), ("r", "y", "c", "h", "x"))
    return jax.shard_map(
        local,
        mesh=fine,
        in_specs=(
            P(("r", "h", "x"), ("y", "c")),
            P("r", ("y", "c")),
            P("r", ("y", "c")),
            P(("r", "h", "x"), ("y", "c")),
        ),
        out_specs=(
            P(("r", "h", "x"), ("y", "c")),
            P(("y", "c", "h", "x"), "r"),
            P("r", ("y", "c", "h", "x")),
            P("r", ("y", "c", "h", "x")),
        ),
        check_vma=False,
    )
```

```python
import functools

import jax
import jax.numpy as jnp
from jax import lax
from jax.experimental import pallas as pl
from jax.experimental.pallas import tpu as pltpu
from jax.sharding import Mesh, PartitionSpec as P

RING = 16
ROWS = 8
FORWARD = ((3, -1), (3, 0), (3, 1), (0, -1), (0, 0), (0, 1), (-3, -1), (-3, 0))
BACKWARD = ((-3, 0), (-2, 0), (-1, 0), (0, 0), (1, 0), (2, 0), (3, 0), (3, -1))


def ring_index(z):
    z %= RING
    return (z % ROWS) * 2 + z // ROWS


def ring_shift(value, step):
    pairs = [(ring_index(z), ring_index(z + step)) for z in range(RING)]
    return lax.ppermute(value, ("r", "h"), pairs)


def place(z, col):
    z %= RING
    return ((z % ROWS) * ROWS + col) * 2 + z // ROWS


def slot(at):
    return (at % 4) * 2 + at // 4


def token_pairs():
    pairs = []
    for z in range(RING):
        for at, (ahead, block) in enumerate(FORWARD):
            pairs.append((place(z + ahead, (z + block) % ROWS), place(z, slot(at))))
    return pairs


def result_pairs():
    pairs = []
    for z in range(RING):
        for at, (ahead, block) in enumerate(BACKWARD):
            tile = (z + ahead) % RING
            row = (z + block) % ROWS
            pairs.append((place(z, slot(at)), place(row + ROWS * (tile // ROWS), tile % ROWS)))
    return pairs


def dot_f32(left, right, dims=((1,), (0,))):
    return lax.dot_general(left, right, (dims, ((), ())), preferred_element_type=jnp.float32)


SMEM_SPEC = pl.BlockSpec(memory_space=pltpu.SMEM)
VMEM_SPEC = pl.BlockSpec(memory_space=pltpu.VMEM)
PARAMS = pltpu.CompilerParams(vmem_limit_bytes=16 << 20)


def swap_cores(value):
    return lax.ppermute(value, "c", [(0, 1), (1, 0)])


def join_cores(core, own_ref, other_ref, both_ref):
    rows = own_ref.shape[0]
    both_ref[pl.ds(pl.multiple_of(core * rows, rows), rows), :] = own_ref[...]
    both_ref[pl.ds(pl.multiple_of((1 - core) * rows, rows), rows), :] = other_ref[...]


def tile_product(tokens_ref, ats, weights_refs):
    total = 0.0
    for at, weights_ref in zip(ats, weights_refs):
        total = total + dot_f32(tokens_ref[at * 128 : (at + 1) * 128, :], weights_ref[...])
    return total.T


def sends_kernel(core_ref, own_ref, other_ref, below_ref, here_ref, above_ref, up_ref, down_ref, tokens_ref):
    join_cores(core_ref[0], own_ref, other_ref, tokens_ref)
    weights_refs = (below_ref, here_ref, above_ref)
    up_ref[...] = tile_product(tokens_ref, (0, 1, 2), weights_refs).astype(jnp.bfloat16)
    down_ref[...] = tile_product(tokens_ref, (6, 7), weights_refs).astype(jnp.bfloat16)


def own_kernel(core_ref, own_ref, other_ref, below_ref, here_ref, above_ref, out_ref, *refs):
    tokens_ref = refs[-1]
    join_cores(core_ref[0], own_ref, other_ref, tokens_ref)
    out_ref[...] = tile_product(tokens_ref, (3, 4, 5), (below_ref, here_ref, above_ref))
    for tokens_out_ref, ats in zip(refs, ((0, 3, 6), (2, 5), (7, 4, 1))):
        for row, at in enumerate(ats):
            tokens_out_ref[row * 128 : (row + 1) * 128, :] = tokens_ref[at * 128 : (at + 1) * 128, :]


def forward(kernel, outs, core, own, other, weights):
    return pl.pallas_call(
        kernel,
        in_specs=[SMEM_SPEC] + [VMEM_SPEC] * 5,
        out_specs=[VMEM_SPEC] * len(outs),
        out_shape=outs,
        scratch_shapes=[pltpu.VMEM((ROWS * 128, own.shape[1]), jnp.bfloat16)],
        compiler_params=PARAMS,
    )(core, own, other, *weights)


def forward_sends(core, own, other, weights):
    tile = jax.ShapeDtypeStruct((weights[0].shape[1], 128), jnp.bfloat16)
    return forward(sends_kernel, [tile, tile], core, own, other, weights)


def own_sums(core, own, other, weights):
    features, cols = weights[0].shape
    outs = [jax.ShapeDtypeStruct((cols, 128), jnp.float32)]
    outs += [jax.ShapeDtypeStruct((128 * count, features), jnp.bfloat16) for count in (3, 2, 3)]
    return forward(own_kernel, outs, core, own, other, weights)


def pointwise_kernel(total_ref, below_ref, above_ref, cotangent_ref, grads_ref, hidden_ref):
    part = total_ref.shape[0] // 4
    total = total_ref[...] + below_ref[...].astype(jnp.float32) + above_ref[...].astype(jnp.float32)
    for at in range(2):
        gate = total[2 * at * part : (2 * at + 1) * part, :]
        up = total[(2 * at + 1) * part : (2 * at + 2) * part, :]
        cotangent = cotangent_ref[at * part : (at + 1) * part, :].astype(jnp.float32)
        sigmoid = jax.nn.sigmoid(gate)
        silu = gate * sigmoid
        hidden_ref[at * part : (at + 1) * part, :] = (silu * up).astype(jnp.bfloat16)
        grad_gate = cotangent * up * sigmoid * (1.0 + gate * (1.0 - sigmoid))
        grads_ref[2 * at * part : (2 * at + 1) * part, :] = grad_gate.astype(jnp.bfloat16)
        grads_ref[(2 * at + 1) * part : (2 * at + 2) * part, :] = (cotangent * silu).astype(jnp.bfloat16)


def pointwise(total, below, above, cotangent):
    return pl.pallas_call(
        pointwise_kernel,
        in_specs=[VMEM_SPEC] * 4,
        out_specs=[VMEM_SPEC] * 2,
        out_shape=[
            jax.ShapeDtypeStruct(total.shape, jnp.bfloat16),
            jax.ShapeDtypeStruct(cotangent.shape, jnp.bfloat16),
        ],
        compiler_params=PARAMS,
        cost_estimate=pl.CostEstimate(flops=20_000_000_000, bytes_accessed=2_000_000, transcendentals=57344),
    )(total, below, above, cotangent)


def near_kernel(weights_ref, mine_ref, right_ref, left_ref, *refs):
    tile_refs = refs[:5]
    terms_ref, sums_ref, tokens_ref, wide_ref = refs[5:]
    sources = ((right_ref, 2), (left_ref, 1), (mine_ref, 1), (right_ref, 1), (left_ref, 0))
    for at, (tile_ref, (source_ref, row)) in enumerate(zip(tile_refs, sources)):
        tokens_ref[at * 128 : (at + 1) * 128, :] = source_ref[row * 128 : (row + 1) * 128, :]
        wide_ref[:, at * 128 : (at + 1) * 128] = tile_ref[...]
        product = dot_f32(weights_ref[...], tile_ref[...])
        terms_ref[at * 128 : (at + 1) * 128, :] = product.T.astype(jnp.bfloat16)
    sums_ref[...] = dot_f32(wide_ref[...], tokens_ref[...])


def near_products(weights, mine, right, left, tiles):
    features, cols = weights.shape
    return pl.pallas_call(
        near_kernel,
        in_specs=[VMEM_SPEC] * 9,
        out_specs=[VMEM_SPEC] * 2,
        out_shape=[
            jax.ShapeDtypeStruct((5 * 128, features), jnp.bfloat16),
            jax.ShapeDtypeStruct((cols, features), jnp.float32),
        ],
        scratch_shapes=[
            pltpu.VMEM((5 * 128, features), jnp.bfloat16),
            pltpu.VMEM((cols, 5 * 128), jnp.bfloat16),
        ],
        compiler_params=PARAMS,
    )(weights, mine, right, left, *tiles)


def third_kernel(here_ref, below_ref, mine_ref, terms_ref, sums_ref, low_ref, high_ref, *refs):
    all_ref, out_ref, tokens_ref, wide_ref = refs
    for at in range(1, 6):
        all_ref[slot(at) * 128 : (slot(at) + 1) * 128, :] = terms_ref[(at - 1) * 128 : at * 128, :]
    for at, tile_ref, weights_ref in ((0, low_ref, here_ref), (6, high_ref, here_ref), (7, high_ref, below_ref)):
        product = dot_f32(weights_ref[...], tile_ref[...])
        all_ref[slot(at) * 128 : (slot(at) + 1) * 128, :] = product.T.astype(jnp.bfloat16)
    tokens_ref[0:128, :] = mine_ref[0:128, :]
    tokens_ref[128:256, :] = mine_ref[256:384, :]
    wide_ref[:, 0:128] = low_ref[...]
    wide_ref[:, 128:256] = high_ref[...]
    out_ref[...] = sums_ref[...] + dot_f32(wide_ref[...], tokens_ref[...])


def third_products(here, below, mine, terms, sums, low, high):
    features, cols = here.shape
    return pl.pallas_call(
        third_kernel,
        in_specs=[VMEM_SPEC] * 7,
        out_specs=[VMEM_SPEC] * 2,
        out_shape=[
            jax.ShapeDtypeStruct((ROWS * 128, features), jnp.bfloat16),
            jax.ShapeDtypeStruct((cols, features), jnp.float32),
        ],
        scratch_shapes=[
            pltpu.VMEM((256, features), jnp.bfloat16),
            pltpu.VMEM((cols, 256), jnp.bfloat16),
        ],
        compiler_params=PARAMS,
    )(here, below, mine, terms, sums, low, high)


def last_kernel(half_ref, right_ref, sums_ref, tile_ref, keep_ref, send_ref):
    rows = keep_ref.shape[0]
    half = half_ref[0]
    send_rows = pl.ds(pl.multiple_of((1 - half) * rows, 16), rows)
    keep_rows = pl.ds(pl.multiple_of(half * rows, 16), rows)
    tokens = right_ref[0:128, :]
    send = sums_ref[send_rows, :] + dot_f32(tile_ref[send_rows, :], tokens)
    send_ref[...] = send.astype(jnp.bfloat16)
    keep_ref[...] = sums_ref[keep_rows, :] + dot_f32(tile_ref[keep_rows, :], tokens)


def last_sums(half, right, sums, tile):
    cols, features = sums.shape
    shape = (cols // 2, features)
    return pl.pallas_call(
        last_kernel,
        in_specs=[SMEM_SPEC] + [VMEM_SPEC] * 3,
        out_specs=[VMEM_SPEC] * 2,
        out_shape=[jax.ShapeDtypeStruct(shape, jnp.float32), jax.ShapeDtypeStruct(shape, jnp.bfloat16)],
        compiler_params=PARAMS,
    )(half, right, sums, tile)


def local(tokens, gate_weight, up_weight, grad_hidden):
    own_x = lax.axis_index("x")
    core = lax.axis_index("c").astype(jnp.int32).reshape(1)
    half = lax.axis_index("h").astype(jnp.int32).reshape(1)
    features, hidden_cols = gate_weight.shape
    part = hidden_cols // 8

    def own_columns(weight, which):
        return lax.dynamic_slice(weight, (0, (which * 4 + own_x) * part), (features, part))

    weights = jnp.concatenate(
        [own_columns(weight, which) for which in (0, 1) for weight in (gate_weight, up_weight)], 1
    )

    piece = lax.ppermute(tokens, ("r", "y", "c", "h"), token_pairs())
    below = ring_shift(weights, 1)
    above = ring_shift(weights, -1)
    copies = jnp.broadcast_to(piece[None], (16,) + piece.shape)
    own_tokens = lax.all_to_all(copies, ("y", "x"), split_axis=0, concat_axis=0, tiled=True)
    own_tokens = own_tokens.reshape(-1, features)
    cotangent = grad_hidden.reshape(-1, 2, 4, part).transpose(2, 0, 1, 3)
    own_tokens, cotangent, below, above = lax.optimization_barrier((own_tokens, cotangent, below, above))
    other_tokens = swap_cores(own_tokens)
    rows = (below, weights, above)
    up, down = forward_sends(core, own_tokens, other_tokens, rows)
    from_below = ring_shift(up, 3)
    from_above = ring_shift(down, -3)
    cotangent = lax.all_to_all(cotangent, "x", split_axis=0, concat_axis=0, tiled=True)
    cotangent = cotangent.reshape(-1, 2 * part).T
    total, to_left, to_right, mine = own_sums(core, own_tokens, other_tokens, rows)
    right_tokens = ring_shift(to_left, -1)
    left_tokens = ring_shift(to_right, 1)
    grads, hidden = pointwise(total, from_below, from_above, cotangent)
    grads, right_tokens, left_tokens = lax.optimization_barrier((grads, right_tokens, left_tokens))

    left_1 = ring_shift(grads, -1)
    right_1 = ring_shift(grads, 1)
    left_2 = ring_shift(left_1, -1)
    right_2 = ring_shift(right_1, 1)
    left_3 = ring_shift(left_2, -1)
    right_3 = ring_shift(right_2, 1)
    terms, sums = near_products(
        weights, mine, right_tokens, left_tokens, [right_2, right_1, grads, left_1, left_2]
    )
    left_3, right_3, terms, sums = lax.optimization_barrier((left_3, right_3, terms, sums))
    left_4 = ring_shift(left_3, -1)
    terms, sums = third_products(weights, below, mine, terms, sums, right_3, left_3)
    left_4, terms = lax.optimization_barrier((left_4, terms))
    terms = lax.all_to_all(
        terms.reshape(32, -1, features), ("y", "c", "x"), split_axis=0, concat_axis=0, tiled=True
    )
    keep, send = last_sums(half, right_tokens, sums, left_4)
    received = lax.ppermute(send, "h", [(0, 1), (1, 0)])
    grad_tokens = jnp.sum(terms.astype(jnp.float32), 0).astype(jnp.bfloat16)
    grad_tokens, hidden = lax.optimization_barrier((grad_tokens, hidden))
    hidden = lax.all_to_all(
        hidden.T.reshape(-1, 2, 1, part), "x", split_axis=0, concat_axis=2, tiled=True
    )
    grad_tokens = lax.ppermute(grad_tokens, ("r", "y", "c", "h"), result_pairs())
    grad_tokens, hidden, keep = lax.optimization_barrier((grad_tokens, hidden, keep))
    grad_weights = keep + received.astype(jnp.float32)
    return hidden.reshape(-1, hidden_cols), grad_tokens, grad_weights[:part].T, grad_weights[part:].T


def solution(mesh):
    fine = Mesh(mesh.devices.reshape(8, 4, 2, 2, 4), ("r", "y", "c", "h", "x"))
    return jax.shard_map(
        local,
        mesh=fine,
        in_specs=(
            P(("r", "h", "x"), ("y", "c")),
            P("r", ("y", "c")),
            P("r", ("y", "c")),
            P(("r", "h", "x"), ("y", "c")),
        ),
        out_specs=(
            P(("r", "h", "x"), ("y", "c")),
            P(("y", "c", "h", "x"), "r"),
            P("r", ("y", "c", "h", "x")),
            P("r", ("y", "c", "h", "x")),
        ),
        check_vma=False,
    )
```

```python
import functools

import jax
import jax.numpy as jnp
from jax import lax
from jax.experimental import pallas as pl
from jax.experimental.pallas import tpu as pltpu
from jax.sharding import Mesh, PartitionSpec as P

RING = 16
ROWS = 8
BEFORE = 3


def ring_index(z):
    z %= RING
    return (z % ROWS) * 2 + z // ROWS


def ring_shift(value, step):
    pairs = [(ring_index(z), ring_index(z + step)) for z in range(RING)]
    return lax.ppermute(value, ("r", "h"), pairs)


def place(z, col):
    z %= RING
    return ((z % ROWS) * ROWS + col) * 2 + z // ROWS


def slot(offset):
    return (offset % 4) * 2 + offset // 4


def token_pairs():
    pairs = []
    for z in range(RING):
        for offset in range(ROWS):
            pairs.append((place(z + offset - BEFORE, z % ROWS), place(z, slot(offset))))
    return pairs


def result_pairs():
    pairs = []
    for z in range(RING):
        for offset in range(ROWS):
            tile = (z + offset - BEFORE) % RING
            pairs.append((place(z, slot(offset)), place(z % ROWS + ROWS * (tile // ROWS), tile % ROWS)))
    return pairs


def dot_f32(left, right, dims=((1,), (0,))):
    return lax.dot_general(left, right, (dims, ((), ())), preferred_element_type=jnp.float32)


ANY_SPEC = pl.BlockSpec(memory_space=pl.ANY)
SMEM_SPEC = pl.BlockSpec(memory_space=pltpu.SMEM)
VMEM_SPEC = pl.BlockSpec(memory_space=pltpu.VMEM)
PARAMS = pltpu.CompilerParams(vmem_limit_bytes=16 << 20)


def swap_cores(value):
    return lax.ppermute(value, "c", [(0, 1), (1, 0)])


def join_cores(core, own_ref, other_ref, both_ref):
    rows = own_ref.shape[0]
    both_ref[pl.ds(pl.multiple_of(core * rows, rows), rows), :] = own_ref[...]
    both_ref[pl.ds(pl.multiple_of((1 - core) * rows, rows), rows), :] = other_ref[...]


def forward_kernel(offsets, core_ref, own_ref, other_ref, weights_ref, *refs):
    tokens_ref = refs[-1]
    join_cores(core_ref[0], own_ref, other_ref, tokens_ref)
    for offset, tile_ref in zip(offsets, refs):
        product = dot_f32(tokens_ref[offset * 128 : (offset + 1) * 128, :], weights_ref[...])
        tile_ref[...] = product.T.astype(jnp.bfloat16)


def forward_tiles(offsets, core, own, other, weights):
    features, cols = weights.shape
    return pl.pallas_call(
        functools.partial(forward_kernel, offsets),
        in_specs=[SMEM_SPEC] + [VMEM_SPEC] * 3,
        out_specs=[VMEM_SPEC] * len(offsets),
        out_shape=[jax.ShapeDtypeStruct((cols, 128), jnp.bfloat16)] * len(offsets),
        scratch_shapes=[pltpu.VMEM((ROWS * 128, features), jnp.bfloat16)],
        compiler_params=PARAMS,
    )(core, own, other, weights)


def term_rows(at):
    return [((at % 4 * 4 + x) * 2 + at // 4) * 32 for x in range(4)]


def near_kernel(core_ref, own_ref, other_ref, weights_ref, *refs):
    tile_refs = refs[:7]
    terms_ref, sums_ref, tokens_ref, wide_ref = refs[7:]
    join_cores(core_ref[0], own_ref, other_ref, tokens_ref)
    for at, tile_ref in enumerate(tile_refs):
        wide_ref[:, at * 128 : (at + 1) * 128] = tile_ref[...]
        product = dot_f32(weights_ref[...], tile_ref[...]).T.astype(jnp.bfloat16)
        for part, first in enumerate(term_rows(at)):
            terms_ref[first : first + 32, :] = product[part * 32 : (part + 1) * 32, :]
    for first in term_rows(7):
        terms_ref[first : first + 32, :] = jnp.zeros((32, terms_ref.shape[1]), jnp.bfloat16)
    sums_ref[...] = dot_f32(wide_ref[...], tokens_ref[0:896, :])


def near_products(core, own, other, weights, tiles):
    features, cols = weights.shape
    return pl.pallas_call(
        near_kernel,
        in_specs=[SMEM_SPEC] + [VMEM_SPEC] * 10,
        out_specs=[VMEM_SPEC] * 2,
        out_shape=[
            jax.ShapeDtypeStruct((ROWS * 128, features), jnp.bfloat16),
            jax.ShapeDtypeStruct((cols, features), jnp.float32),
        ],
        scratch_shapes=[
            pltpu.VMEM((ROWS * 128, features), jnp.bfloat16),
            pltpu.VMEM((cols, 7 * 128), jnp.bfloat16),
        ],
        compiler_params=PARAMS,
    )(core, own, other, weights, *tiles)


def last_sums_kernel(core_ref, half_ref, own_ref, other_ref, sums_ref, tile_ref, keep_ref, send_ref, last_ref):
    rows = own_ref.shape[0]

    @pl.when(core_ref[0] == 0)
    def _():
        last_ref[...] = other_ref[rows - 128 :, :]

    @pl.when(core_ref[0] == 1)
    def _():
        last_ref[...] = own_ref[rows - 128 :, :]

    rows = keep_ref.shape[0]
    half = half_ref[0]
    send_rows = pl.ds(pl.multiple_of((1 - half) * rows, 16), rows)
    keep_rows = pl.ds(pl.multiple_of(half * rows, 16), rows)
    send = sums_ref[send_rows, :] + dot_f32(tile_ref[send_rows, :], last_ref[...])
    send_ref[...] = send.astype(jnp.bfloat16)
    keep_ref[...] = sums_ref[keep_rows, :] + dot_f32(tile_ref[keep_rows, :], last_ref[...])


def last_sums(core, half, own, other, sums, tile):
    cols, features = sums.shape
    return pl.pallas_call(
        last_sums_kernel,
        in_specs=[SMEM_SPEC] * 2 + [VMEM_SPEC] * 4,
        out_specs=[VMEM_SPEC] * 2,
        out_shape=[
            jax.ShapeDtypeStruct((cols // 2, features), jnp.float32),
            jax.ShapeDtypeStruct((cols // 2, features), jnp.bfloat16),
        ],
        scratch_shapes=[pltpu.VMEM((128, features), jnp.bfloat16)],
        compiler_params=PARAMS,
    )(core, half, own, other, sums, tile)


def last_terms_kernel(weights_ref, tile_ref, terms_ref, all_ref, block_ref, sem_ref):
    del terms_ref
    block_ref[...] = dot_f32(weights_ref[...], tile_ref[...]).T.astype(jnp.bfloat16)
    copies = [
        pltpu.make_async_copy(
            block_ref.at[part * 32 : (part + 1) * 32, :], all_ref.at[first : first + 32, :], sem_ref.at[part]
        )
        for part, first in enumerate(term_rows(7))
    ]
    for copy in copies:
        copy.start()
    for copy in copies:
        copy.wait()


def last_terms(weights, terms, tile):
    return pl.pallas_call(
        last_terms_kernel,
        in_specs=[VMEM_SPEC] * 2 + [ANY_SPEC],
        out_specs=ANY_SPEC,
        out_shape=jax.ShapeDtypeStruct(terms.shape, terms.dtype),
        input_output_aliases={2: 0},
        scratch_shapes=[pltpu.VMEM((128, terms.shape[1]), jnp.bfloat16), pltpu.SemaphoreType.DMA((4,))],
        compiler_params=PARAMS,
    )(weights, tile, terms)


def total_kernel(core_ref, parts_ref, keep_ref, send_ref, total_ref):
    total_ref[...] = jnp.sum(parts_ref[...].astype(jnp.float32), 0)
    rows = keep_ref.shape[0]
    core = core_ref[0]
    keep_ref[...] = total_ref[pl.ds(pl.multiple_of(core * rows, rows), rows), :]
    send = total_ref[pl.ds(pl.multiple_of((1 - core) * rows, rows), rows), :]
    send_ref[...] = send.astype(jnp.bfloat16)


def sum_parts(core, parts):
    _, rows, features = parts.shape
    shape = (rows // 2, features)
    return pl.pallas_call(
        total_kernel,
        in_specs=[SMEM_SPEC, VMEM_SPEC],
        out_specs=[VMEM_SPEC] * 2,
        out_shape=[jax.ShapeDtypeStruct(shape, jnp.float32), jax.ShapeDtypeStruct(shape, jnp.bfloat16)],
        scratch_shapes=[pltpu.VMEM((rows, features), jnp.float32)],
        compiler_params=PARAMS,
    )(core, parts)


def add_tiles(*tiles):
    return sum(tile.astype(jnp.float32) for tile in tiles).astype(jnp.bfloat16)


def local(tokens, gate_weight, up_weight, grad_hidden):
    own_x = lax.axis_index("x")
    core = lax.axis_index("c").astype(jnp.int32).reshape(1)
    half = lax.axis_index("h").astype(jnp.int32).reshape(1)
    features, hidden_cols = gate_weight.shape
    part = hidden_cols // 8

    def own_columns(weight, which):
        return lax.dynamic_slice(weight, (0, (which * 4 + own_x) * part), (features, part))

    weights = jnp.concatenate(
        [own_columns(weight, which) for which in (0, 1) for weight in (gate_weight, up_weight)], 1
    )

    piece = lax.ppermute(tokens, ("r", "y", "c", "h"), token_pairs())
    copies = jnp.broadcast_to(piece[None], (16,) + piece.shape)
    own_tokens = lax.all_to_all(copies, ("y", "x"), split_axis=0, concat_axis=0, tiled=True)
    own_tokens = own_tokens.reshape(-1, features)
    cotangent = grad_hidden.reshape(-1, 2, 4, part).transpose(2, 0, 1, 3)
    own_tokens, cotangent, weights = lax.optimization_barrier((own_tokens, cotangent, weights))
    other_tokens = swap_cores(own_tokens)
    cotangent = lax.all_to_all(cotangent, "x", split_axis=0, concat_axis=0, tiled=True)
    partial = {}
    for offsets in ((7, 0), (6, 1, 5, 2, 4, 3)):
        partial.update(zip(offsets, forward_tiles(offsets, core, own_tokens, other_tokens, weights)))
    right = ring_shift(partial[7], 1)
    left = ring_shift(partial[0], -1)
    right = add_tiles(right, partial[6])
    left = add_tiles(left, partial[1])
    right = add_tiles(ring_shift(right, 1), partial[5])
    left = add_tiles(ring_shift(left, -1), partial[2])
    right = add_tiles(ring_shift(right, 1), partial[4])
    left = ring_shift(left, -1)
    right, cotangent = lax.optimization_barrier((right, cotangent))
    right = ring_shift(right, 1)
    cotangent = cotangent.reshape(-1, 2 * part).T.astype(jnp.float32)
    total = partial[BEFORE].astype(jnp.float32) + left.astype(jnp.float32) + right.astype(jnp.float32)
    gate_pre = jnp.concatenate([total[:part], total[2 * part : 3 * part]], 0)
    up_pre = jnp.concatenate([total[part : 2 * part], total[3 * part :]], 0)

    sigmoid = jax.nn.sigmoid(gate_pre)
    silu = gate_pre * sigmoid
    hidden = (silu * up_pre).astype(jnp.bfloat16)
    grad_gate = (cotangent * up_pre * sigmoid * (1.0 + gate_pre * (1.0 - sigmoid))).astype(jnp.bfloat16)
    grad_up = (cotangent * silu).astype(jnp.bfloat16)
    grads = jnp.concatenate([grad_gate[:part], grad_up[:part], grad_gate[part:], grad_up[part:]], 0)

    left_1 = ring_shift(grads, -1)
    right_1 = ring_shift(grads, 1)
    left_2 = ring_shift(left_1, -1)
    right_2 = ring_shift(right_1, 1)
    left_3 = ring_shift(left_2, -1)
    right_3 = ring_shift(right_2, 1)
    left_4 = ring_shift(left_3, -1)
    terms, sums = near_products(
        core, own_tokens, other_tokens, weights, [right_3, right_2, right_1, grads, left_1, left_2, left_3]
    )
    keep, send = last_sums(core, half, own_tokens, other_tokens, sums, left_4)
    terms, send = lax.optimization_barrier((terms, send))
    received = lax.ppermute(send, "h", [(0, 1), (1, 0)])
    terms = last_terms(weights, terms, left_4)
    terms = lax.all_to_all(
        terms.reshape(16, -1, features), ("y", "x"), split_axis=0, concat_axis=0, tiled=True
    )
    keep_terms, send_terms = sum_parts(core, terms)
    grad_tokens = (keep_terms + swap_cores(send_terms).astype(jnp.float32)).astype(jnp.bfloat16)
    grad_tokens, hidden = lax.optimization_barrier((grad_tokens, hidden))
    hidden = lax.all_to_all(
        hidden.T.reshape(-1, 2, 1, part), "x", split_axis=0, concat_axis=2, tiled=True
    )
    grad_tokens = lax.ppermute(grad_tokens, ("r", "y", "c", "h"), result_pairs())
    grad_tokens, hidden, keep = lax.optimization_barrier((grad_tokens, hidden, keep))
    grad_weights = keep + received.astype(jnp.float32)
    return hidden.reshape(-1, hidden_cols), grad_tokens, grad_weights[:part].T, grad_weights[part:].T


def solution(mesh):
    fine = Mesh(mesh.devices.reshape(8, 4, 2, 2, 4), ("r", "y", "c", "h", "x"))
    return jax.shard_map(
        local,
        mesh=fine,
        in_specs=(
            P(("r", "h", "x"), ("y", "c")),
            P("r", ("y", "c")),
            P("r", ("y", "c")),
            P(("r", "h", "x"), ("y", "c")),
        ),
        out_specs=(
            P(("r", "h", "x"), ("y", "c")),
            P(("y", "c", "h", "x"), "r"),
            P("r", ("y", "c", "h", "x")),
            P("r", ("y", "c", "h", "x")),
        ),
        check_vma=False,
    )
```

```python
import functools

import jax
import jax.numpy as jnp
from jax import lax
from jax.experimental import pallas as pl
from jax.experimental.pallas import tpu as pltpu
from jax.sharding import Mesh, PartitionSpec as P

RING = 16
ROWS = 8
BEFORE = 3


def ring_index(z):
    z %= RING
    return (z % ROWS) * 2 + z // ROWS


def ring_shift(value, step):
    pairs = [(ring_index(z), ring_index(z + step)) for z in range(RING)]
    return lax.ppermute(value, ("r", "h"), pairs)


def place(z, col):
    z %= RING
    return ((z % ROWS) * ROWS + col) * 2 + z // ROWS


def slot(offset):
    return (offset % 4) * 2 + offset // 4


def token_pairs():
    pairs = []
    for z in range(RING):
        for offset in range(ROWS):
            pairs.append((place(z + offset - BEFORE, z % ROWS), place(z, slot(offset))))
    return pairs


def result_pairs():
    pairs = []
    for z in range(RING):
        for offset in range(ROWS):
            tile = (z + offset - BEFORE) % RING
            pairs.append((place(z, slot(offset)), place(z % ROWS + ROWS * (tile // ROWS), tile % ROWS)))
    return pairs


def dot_f32(left, right, dims=((1,), (0,))):
    return lax.dot_general(left, right, (dims, ((), ())), preferred_element_type=jnp.float32)


ANY_SPEC = pl.BlockSpec(memory_space=pl.ANY)
SMEM_SPEC = pl.BlockSpec(memory_space=pltpu.SMEM)
VMEM_SPEC = pl.BlockSpec(memory_space=pltpu.VMEM)
PARAMS = pltpu.CompilerParams(vmem_limit_bytes=16 << 20)


def swap_cores(value):
    return lax.ppermute(value, "c", [(0, 1), (1, 0)])


def join_cores(core, own_ref, other_ref, both_ref):
    rows = own_ref.shape[0]
    both_ref[pl.ds(pl.multiple_of(core * rows, rows), rows), :] = own_ref[...]
    both_ref[pl.ds(pl.multiple_of((1 - core) * rows, rows), rows), :] = other_ref[...]


def forward_kernel(offsets, core_ref, own_ref, other_ref, weights_ref, *refs):
    tokens_ref = refs[-1]
    join_cores(core_ref[0], own_ref, other_ref, tokens_ref)
    for offset, tile_ref in zip(offsets, refs):
        product = dot_f32(tokens_ref[offset * 128 : (offset + 1) * 128, :], weights_ref[...])
        tile_ref[...] = product.T.astype(jnp.bfloat16)


def forward_tiles(offsets, core, own, other, weights):
    features, cols = weights.shape
    return pl.pallas_call(
        functools.partial(forward_kernel, offsets),
        in_specs=[SMEM_SPEC] + [VMEM_SPEC] * 3,
        out_specs=[VMEM_SPEC] * len(offsets),
        out_shape=[jax.ShapeDtypeStruct((cols, 128), jnp.bfloat16)] * len(offsets),
        scratch_shapes=[pltpu.VMEM((ROWS * 128, features), jnp.bfloat16)],
        compiler_params=PARAMS,
    )(core, own, other, weights)


def term_rows(at):
    return [((at % 4 * 4 + x) * 2 + at // 4) * 32 for x in range(4)]


def near_kernel(core_ref, own_ref, other_ref, weights_ref, *refs):
    tile_refs = refs[:7]
    terms_ref, sums_ref, tokens_ref, wide_ref = refs[7:]
    join_cores(core_ref[0], own_ref, other_ref, tokens_ref)
    for at, tile_ref in enumerate(tile_refs):
        wide_ref[:, at * 128 : (at + 1) * 128] = tile_ref[...]
        product = dot_f32(weights_ref[...], tile_ref[...]).T.astype(jnp.bfloat16)
        for part, first in enumerate(term_rows(at)):
            terms_ref[first : first + 32, :] = product[part * 32 : (part + 1) * 32, :]
    for first in term_rows(7):
        terms_ref[first : first + 32, :] = jnp.zeros((32, terms_ref.shape[1]), jnp.bfloat16)
    sums_ref[...] = dot_f32(wide_ref[...], tokens_ref[0:896, :])


def near_products(core, own, other, weights, tiles):
    features, cols = weights.shape
    return pl.pallas_call(
        near_kernel,
        in_specs=[SMEM_SPEC] + [VMEM_SPEC] * 10,
        out_specs=[VMEM_SPEC] * 2,
        out_shape=[
            jax.ShapeDtypeStruct((ROWS * 128, features), jnp.bfloat16),
            jax.ShapeDtypeStruct((cols, features), jnp.float32),
        ],
        scratch_shapes=[
            pltpu.VMEM((ROWS * 128, features), jnp.bfloat16),
            pltpu.VMEM((cols, 7 * 128), jnp.bfloat16),
        ],
        compiler_params=PARAMS,
    )(core, own, other, weights, *tiles)


def last_sums_kernel(core_ref, half_ref, own_ref, other_ref, sums_ref, tile_ref, keep_ref, send_ref, last_ref):
    rows = own_ref.shape[0]

    @pl.when(core_ref[0] == 0)
    def _():
        last_ref[...] = other_ref[rows - 128 :, :]

    @pl.when(core_ref[0] == 1)
    def _():
        last_ref[...] = own_ref[rows - 128 :, :]

    rows = keep_ref.shape[0]
    half = half_ref[0]
    send_rows = pl.ds(pl.multiple_of((1 - half) * rows, 16), rows)
    keep_rows = pl.ds(pl.multiple_of(half * rows, 16), rows)
    send = sums_ref[send_rows, :] + dot_f32(tile_ref[send_rows, :], last_ref[...])
    send_ref[...] = send.astype(jnp.bfloat16)
    keep_ref[...] = sums_ref[keep_rows, :] + dot_f32(tile_ref[keep_rows, :], last_ref[...])


def last_sums(core, half, own, other, sums, tile):
    cols, features = sums.shape
    return pl.pallas_call(
        last_sums_kernel,
        in_specs=[SMEM_SPEC] * 2 + [VMEM_SPEC] * 4,
        out_specs=[VMEM_SPEC] * 2,
        out_shape=[
            jax.ShapeDtypeStruct((cols // 2, features), jnp.float32),
            jax.ShapeDtypeStruct((cols // 2, features), jnp.bfloat16),
        ],
        scratch_shapes=[pltpu.VMEM((128, features), jnp.bfloat16)],
        compiler_params=PARAMS,
    )(core, half, own, other, sums, tile)


def last_terms_kernel(weights_ref, tile_ref, terms_ref, all_ref, block_ref, sem_ref):
    del terms_ref
    block_ref[...] = dot_f32(weights_ref[...], tile_ref[...]).T.astype(jnp.bfloat16)
    copies = [
        pltpu.make_async_copy(
            block_ref.at[part * 32 : (part + 1) * 32, :], all_ref.at[first : first + 32, :], sem_ref.at[part]
        )
        for part, first in enumerate(term_rows(7))
    ]
    for copy in copies:
        copy.start()
    for copy in copies:
        copy.wait()


def last_terms(weights, terms, tile):
    return pl.pallas_call(
        last_terms_kernel,
        in_specs=[VMEM_SPEC] * 2 + [ANY_SPEC],
        out_specs=ANY_SPEC,
        out_shape=jax.ShapeDtypeStruct(terms.shape, terms.dtype),
        input_output_aliases={2: 0},
        scratch_shapes=[pltpu.VMEM((128, terms.shape[1]), jnp.bfloat16), pltpu.SemaphoreType.DMA((4,))],
        compiler_params=pltpu.CompilerParams(vmem_limit_bytes=6 << 20),
    )(weights, tile, terms)


def total_kernel(core_ref, parts_ref, keep_ref, send_ref, total_ref):
    total_ref[...] = jnp.sum(parts_ref[...].astype(jnp.float32), 0)
    rows = keep_ref.shape[0]
    core = core_ref[0]
    keep_ref[...] = total_ref[pl.ds(pl.multiple_of(core * rows, rows), rows), :]
    send = total_ref[pl.ds(pl.multiple_of((1 - core) * rows, rows), rows), :]
    send_ref[...] = send.astype(jnp.bfloat16)


def finish_kernel(keep_ref, received_ref, gate_ref, up_ref):
    rows = gate_ref.shape[0]
    gate_ref[...] = keep_ref[:rows, :] + received_ref[:rows, :].astype(jnp.float32)
    up_ref[...] = keep_ref[rows:, :] + received_ref[rows:, :].astype(jnp.float32)


def finish(keep, received):
    shape = jax.ShapeDtypeStruct((keep.shape[0] // 2, keep.shape[1]), jnp.float32)
    return pl.pallas_call(
        finish_kernel,
        in_specs=[VMEM_SPEC] * 2,
        out_specs=[VMEM_SPEC] * 2,
        out_shape=[shape, shape],
        compiler_params=PARAMS,
    )(keep, received)


def copy_kernel(in_ref, out_ref):
    out_ref[...] = in_ref[...]


def copied(value, flops):
    return pl.pallas_call(
        copy_kernel,
        in_specs=[VMEM_SPEC],
        out_specs=VMEM_SPEC,
        out_shape=jax.ShapeDtypeStruct(value.shape, value.dtype),
        compiler_params=PARAMS,
        cost_estimate=pl.CostEstimate(flops=flops, bytes_accessed=1, transcendentals=0),
    )(value)


def sum_parts(core, parts):
    _, rows, features = parts.shape
    shape = (rows // 2, features)
    return pl.pallas_call(
        total_kernel,
        in_specs=[SMEM_SPEC, VMEM_SPEC],
        out_specs=[VMEM_SPEC] * 2,
        out_shape=[jax.ShapeDtypeStruct(shape, jnp.float32), jax.ShapeDtypeStruct(shape, jnp.bfloat16)],
        scratch_shapes=[pltpu.VMEM((rows, features), jnp.float32)],
        compiler_params=PARAMS,
    )(core, parts)


def add_tiles(*tiles):
    return sum(tile.astype(jnp.float32) for tile in tiles).astype(jnp.bfloat16)


def local(tokens, gate_weight, up_weight, grad_hidden):
    own_x = lax.axis_index("x")
    core = lax.axis_index("c").astype(jnp.int32).reshape(1)
    half = lax.axis_index("h").astype(jnp.int32).reshape(1)
    features, hidden_cols = gate_weight.shape
    part = hidden_cols // 8

    def own_columns(weight, which):
        return lax.dynamic_slice(weight, (0, (which * 4 + own_x) * part), (features, part))

    weights = jnp.concatenate(
        [own_columns(weight, which) for which in (0, 1) for weight in (gate_weight, up_weight)], 1
    )

    piece = lax.ppermute(tokens, ("r", "y", "c", "h"), token_pairs())
    copies = jnp.broadcast_to(piece[None], (16,) + piece.shape)
    own_tokens = lax.all_to_all(copies, ("y", "x"), split_axis=0, concat_axis=0, tiled=True)
    own_tokens = own_tokens.reshape(-1, features)
    cotangent = grad_hidden.reshape(-1, 2, 4, part).transpose(2, 0, 1, 3)
    own_tokens, cotangent, weights = lax.optimization_barrier((own_tokens, cotangent, weights))
    other_tokens = swap_cores(own_tokens)
    cotangent = lax.all_to_all(cotangent, "x", split_axis=0, concat_axis=0, tiled=True)
    partial = {}
    for offsets in ((7, 0), (6, 1, 5, 2, 4, 3)):
        partial.update(zip(offsets, forward_tiles(offsets, core, own_tokens, other_tokens, weights)))
    right = ring_shift(partial[7], 1)
    left = ring_shift(partial[0], -1)
    right = add_tiles(right, partial[6])
    left = add_tiles(left, partial[1])
    right = add_tiles(ring_shift(right, 1), partial[5])
    left = add_tiles(ring_shift(left, -1), partial[2])
    right = add_tiles(ring_shift(right, 1), partial[4])
    left = ring_shift(left, -1)
    right, cotangent = lax.optimization_barrier((right, cotangent))
    right = ring_shift(right, 1)
    cotangent = cotangent.reshape(-1, 2 * part).T.astype(jnp.float32)
    total = partial[BEFORE].astype(jnp.float32) + left.astype(jnp.float32) + right.astype(jnp.float32)
    gate_pre = jnp.concatenate([total[:part], total[2 * part : 3 * part]], 0)
    up_pre = jnp.concatenate([total[part : 2 * part], total[3 * part :]], 0)

    sigmoid = jax.nn.sigmoid(gate_pre)
    silu = gate_pre * sigmoid
    hidden = (silu * up_pre).astype(jnp.bfloat16)
    grad_gate = (cotangent * up_pre * sigmoid * (1.0 + gate_pre * (1.0 - sigmoid))).astype(jnp.bfloat16)
    grad_up = (cotangent * silu).astype(jnp.bfloat16)
    grads = jnp.concatenate([grad_gate[:part], grad_up[:part], grad_gate[part:], grad_up[part:]], 0)

    left_1 = ring_shift(grads, -1)
    right_1 = ring_shift(grads, 1)
    left_2 = ring_shift(left_1, -1)
    right_2 = ring_shift(right_1, 1)
    left_3 = ring_shift(left_2, -1)
    right_3 = ring_shift(right_2, 1)
    left_4 = ring_shift(left_3, -1)
    terms, sums = near_products(
        core, own_tokens, other_tokens, weights, [right_3, right_2, right_1, grads, left_1, left_2, left_3]
    )
    keep, send = last_sums(core, half, own_tokens, other_tokens, sums, left_4)
    terms, send = lax.optimization_barrier((terms, send))
    received = lax.ppermute(send, "h", [(0, 1), (1, 0)])
    terms = last_terms(weights, terms, left_4)
    terms = lax.all_to_all(
        terms.reshape(16, -1, features), ("y", "x"), split_axis=0, concat_axis=0, tiled=True
    )
    keep_terms, send_terms = sum_parts(core, terms)
    grad_tokens = (keep_terms + swap_cores(send_terms).astype(jnp.float32)).astype(jnp.bfloat16)
    grad_tokens, hidden = lax.optimization_barrier((grad_tokens, hidden))
    hidden = lax.all_to_all(
        hidden.T.reshape(-1, 2, 1, part), "x", split_axis=0, concat_axis=2, tiled=True
    )
    grad_tokens = lax.ppermute(grad_tokens, ("r", "y", "c", "h"), result_pairs())
    grad_tokens = copied(grad_tokens, 1_000_000_000)
    hidden = hidden.reshape(-1, hidden_cols)
    grad_tokens, hidden, keep = lax.optimization_barrier((grad_tokens, hidden, keep))
    gate_grad, up_grad = finish(keep, received)
    return hidden, grad_tokens, gate_grad.T, up_grad.T


def solution(mesh):
    fine = Mesh(mesh.devices.reshape(8, 4, 2, 2, 4), ("r", "y", "c", "h", "x"))
    return jax.shard_map(
        local,
        mesh=fine,
        in_specs=(
            P(("r", "h", "x"), ("y", "c")),
            P("r", ("y", "c")),
            P("r", ("y", "c")),
            P(("r", "h", "x"), ("y", "c")),
        ),
        out_specs=(
            P(("r", "h", "x"), ("y", "c")),
            P(("y", "c", "h", "x"), "r"),
            P("r", ("y", "c", "h", "x")),
            P("r", ("y", "c", "h", "x")),
        ),
        check_vma=False,
    )
```

```python
import functools

import jax
import jax.numpy as jnp
from jax import lax
from jax.experimental import pallas as pl
from jax.experimental.pallas import tpu as pltpu
from jax.sharding import Mesh, PartitionSpec as P

RING = 16
ROWS = 8
BEFORE = 3


def ring_index(z):
    z %= RING
    return (z % ROWS) * 2 + z // ROWS


def ring_shift(value, step):
    pairs = [(ring_index(z), ring_index(z + step)) for z in range(RING)]
    return lax.ppermute(value, ("r", "h"), pairs)


def place(z, col):
    z %= RING
    return ((z % ROWS) * ROWS + col) * 2 + z // ROWS


def slot(offset):
    return (offset % 4) * 2 + offset // 4


def token_pairs():
    pairs = []
    for z in range(RING):
        for offset in range(ROWS):
            pairs.append((place(z + offset - BEFORE, z % ROWS), place(z, slot(offset))))
    return pairs


def result_pairs():
    pairs = []
    for z in range(RING):
        for offset in range(ROWS):
            tile = (z + offset - BEFORE) % RING
            pairs.append((place(z, slot(offset)), place(z % ROWS + ROWS * (tile // ROWS), tile % ROWS)))
    return pairs


def dot_f32(left, right, dims=((1,), (0,))):
    return lax.dot_general(left, right, (dims, ((), ())), preferred_element_type=jnp.float32)


ANY_SPEC = pl.BlockSpec(memory_space=pl.ANY)
SMEM_SPEC = pl.BlockSpec(memory_space=pltpu.SMEM)
VMEM_SPEC = pl.BlockSpec(memory_space=pltpu.VMEM)
PARAMS = pltpu.CompilerParams(vmem_limit_bytes=16 << 20)


def swap_cores(value):
    return lax.ppermute(value, "c", [(0, 1), (1, 0)])


def join_cores(core, own_ref, other_ref, both_ref):
    rows = own_ref.shape[0]
    both_ref[pl.ds(pl.multiple_of(core * rows, rows), rows), :] = own_ref[...]
    both_ref[pl.ds(pl.multiple_of((1 - core) * rows, rows), rows), :] = other_ref[...]


def forward_kernel(offsets, core_ref, own_ref, other_ref, weights_ref, *refs):
    tokens_ref = refs[-1]
    join_cores(core_ref[0], own_ref, other_ref, tokens_ref)
    for offset, tile_ref in zip(offsets, refs):
        product = dot_f32(tokens_ref[offset * 128 : (offset + 1) * 128, :], weights_ref[...])
        tile_ref[...] = product.T.astype(jnp.bfloat16)


def forward_tiles(offsets, core, own, other, weights):
    features, cols = weights.shape
    return pl.pallas_call(
        functools.partial(forward_kernel, offsets),
        in_specs=[SMEM_SPEC] + [VMEM_SPEC] * 3,
        out_specs=[VMEM_SPEC] * len(offsets),
        out_shape=[jax.ShapeDtypeStruct((cols, 128), jnp.bfloat16)] * len(offsets),
        scratch_shapes=[pltpu.VMEM((ROWS * 128, features), jnp.bfloat16)],
        compiler_params=PARAMS,
    )(core, own, other, weights)


def term_rows(at):
    return [((at % 4 * 4 + x) * 2 + at // 4) * 32 for x in range(4)]


def near_kernel(core_ref, own_ref, other_ref, weights_ref, *refs):
    tile_refs = refs[:7]
    terms_ref, sums_ref, tokens_ref, wide_ref = refs[7:]
    join_cores(core_ref[0], own_ref, other_ref, tokens_ref)
    for at, tile_ref in enumerate(tile_refs):
        wide_ref[:, at * 128 : (at + 1) * 128] = tile_ref[...]
        product = dot_f32(weights_ref[...], tile_ref[...]).T.astype(jnp.bfloat16)
        for part, first in enumerate(term_rows(at)):
            terms_ref[first : first + 32, :] = product[part * 32 : (part + 1) * 32, :]
    for first in term_rows(7):
        terms_ref[first : first + 32, :] = jnp.zeros((32, terms_ref.shape[1]), jnp.bfloat16)
    sums_ref[...] = dot_f32(wide_ref[...], tokens_ref[0:896, :])


def near_products(core, own, other, weights, tiles):
    features, cols = weights.shape
    return pl.pallas_call(
        near_kernel,
        in_specs=[SMEM_SPEC] + [VMEM_SPEC] * 10,
        out_specs=[VMEM_SPEC] * 2,
        out_shape=[
            jax.ShapeDtypeStruct((ROWS * 128, features), jnp.bfloat16),
            jax.ShapeDtypeStruct((cols, features), jnp.float32),
        ],
        scratch_shapes=[
            pltpu.VMEM((ROWS * 128, features), jnp.bfloat16),
            pltpu.VMEM((cols, 7 * 128), jnp.bfloat16),
        ],
        compiler_params=PARAMS,
    )(core, own, other, weights, *tiles)


def last_sums_kernel(core_ref, half_ref, own_ref, other_ref, sums_ref, tile_ref, keep_ref, send_ref, last_ref):
    rows = own_ref.shape[0]

    @pl.when(core_ref[0] == 0)
    def _():
        last_ref[...] = other_ref[rows - 128 :, :]

    @pl.when(core_ref[0] == 1)
    def _():
        last_ref[...] = own_ref[rows - 128 :, :]

    rows = keep_ref.shape[0]
    half = half_ref[0]
    send_rows = pl.ds(pl.multiple_of((1 - half) * rows, 16), rows)
    keep_rows = pl.ds(pl.multiple_of(half * rows, 16), rows)
    send = sums_ref[send_rows, :] + dot_f32(tile_ref[send_rows, :], last_ref[...])
    send_ref[...] = send.astype(jnp.bfloat16)
    keep_ref[...] = sums_ref[keep_rows, :] + dot_f32(tile_ref[keep_rows, :], last_ref[...])


def last_sums(core, half, own, other, sums, tile):
    cols, features = sums.shape
    return pl.pallas_call(
        last_sums_kernel,
        in_specs=[SMEM_SPEC] * 2 + [VMEM_SPEC] * 4,
        out_specs=[VMEM_SPEC] * 2,
        out_shape=[
            jax.ShapeDtypeStruct((cols // 2, features), jnp.float32),
            jax.ShapeDtypeStruct((cols // 2, features), jnp.bfloat16),
        ],
        scratch_shapes=[pltpu.VMEM((128, features), jnp.bfloat16)],
        compiler_params=PARAMS,
    )(core, half, own, other, sums, tile)


def last_terms_kernel(weights_ref, tile_ref, terms_ref, all_ref, block_ref, sem_ref):
    del terms_ref
    block_ref[...] = dot_f32(weights_ref[...], tile_ref[...]).T.astype(jnp.bfloat16)
    copies = [
        pltpu.make_async_copy(
            block_ref.at[part * 32 : (part + 1) * 32, :], all_ref.at[first : first + 32, :], sem_ref.at[part]
        )
        for part, first in enumerate(term_rows(7))
    ]
    for copy in copies:
        copy.start()
    for copy in copies:
        copy.wait()


def last_terms(weights, terms, tile):
    return pl.pallas_call(
        last_terms_kernel,
        in_specs=[VMEM_SPEC] * 2 + [ANY_SPEC],
        out_specs=ANY_SPEC,
        out_shape=jax.ShapeDtypeStruct(terms.shape, terms.dtype),
        input_output_aliases={2: 0},
        scratch_shapes=[pltpu.VMEM((128, terms.shape[1]), jnp.bfloat16), pltpu.SemaphoreType.DMA((4,))],
        compiler_params=pltpu.CompilerParams(vmem_limit_bytes=6 << 20),
    )(weights, tile, terms)


def total_kernel(core_ref, parts_ref, keep_ref, send_ref, total_ref):
    total_ref[...] = jnp.sum(parts_ref[...].astype(jnp.float32), 0)
    rows = keep_ref.shape[0]
    core = core_ref[0]
    keep_ref[...] = total_ref[pl.ds(pl.multiple_of(core * rows, rows), rows), :]
    send = total_ref[pl.ds(pl.multiple_of((1 - core) * rows, rows), rows), :]
    send_ref[...] = send.astype(jnp.bfloat16)


def finish_kernel(keep_ref, received_ref, gate_ref, up_ref):
    rows = gate_ref.shape[0]
    gate_ref[...] = keep_ref[:rows, :] + received_ref[:rows, :].astype(jnp.float32)
    up_ref[...] = keep_ref[rows:, :] + received_ref[rows:, :].astype(jnp.float32)


def finish(keep, received):
    shape = jax.ShapeDtypeStruct((keep.shape[0] // 2, keep.shape[1]), jnp.float32)
    return pl.pallas_call(
        finish_kernel,
        in_specs=[VMEM_SPEC] * 2,
        out_specs=[VMEM_SPEC] * 2,
        out_shape=[shape, shape],
        compiler_params=PARAMS,
    )(keep, received)


def copy_kernel(in_ref, out_ref):
    out_ref[...] = in_ref[...]


def copied(value, flops):
    return pl.pallas_call(
        copy_kernel,
        in_specs=[VMEM_SPEC],
        out_specs=VMEM_SPEC,
        out_shape=jax.ShapeDtypeStruct(value.shape, value.dtype),
        compiler_params=PARAMS,
        cost_estimate=pl.CostEstimate(flops=flops, bytes_accessed=1, transcendentals=0),
    )(value)


def sum_parts(core, parts):
    _, rows, features = parts.shape
    shape = (rows // 2, features)
    return pl.pallas_call(
        total_kernel,
        in_specs=[SMEM_SPEC, VMEM_SPEC],
        out_specs=[VMEM_SPEC] * 2,
        out_shape=[jax.ShapeDtypeStruct(shape, jnp.float32), jax.ShapeDtypeStruct(shape, jnp.bfloat16)],
        scratch_shapes=[pltpu.VMEM((rows, features), jnp.float32)],
        compiler_params=PARAMS,
    )(core, parts)


def add_tiles(*tiles):
    return sum(tile.astype(jnp.float32) for tile in tiles).astype(jnp.bfloat16)


def local(tokens, gate_weight, up_weight, grad_hidden):
    own_x = lax.axis_index("x")
    core = lax.axis_index("c").astype(jnp.int32).reshape(1)
    half = lax.axis_index("h").astype(jnp.int32).reshape(1)
    features, hidden_cols = gate_weight.shape
    part = hidden_cols // 8

    def own_columns(weight, which):
        return lax.dynamic_slice(weight, (0, (which * 4 + own_x) * part), (features, part))

    weights = jnp.concatenate(
        [own_columns(weight, which) for which in (0, 1) for weight in (gate_weight, up_weight)], 1
    )

    piece = lax.ppermute(tokens, ("r", "y", "c", "h"), token_pairs())
    copies = jnp.broadcast_to(piece[None], (16,) + piece.shape)
    own_tokens = lax.all_to_all(copies, ("y", "x"), split_axis=0, concat_axis=0, tiled=True)
    own_tokens = own_tokens.reshape(-1, features)
    cotangent = grad_hidden.reshape(-1, 2, 4, part).transpose(2, 0, 1, 3)
    own_tokens, cotangent, weights = lax.optimization_barrier((own_tokens, cotangent, weights))
    other_tokens = swap_cores(own_tokens)
    cotangent = lax.all_to_all(cotangent, "x", split_axis=0, concat_axis=0, tiled=True)
    partial = {}
    for offsets in ((7, 0), (6, 1, 5, 2, 4, 3)):
        partial.update(zip(offsets, forward_tiles(offsets, core, own_tokens, other_tokens, weights)))
    right = ring_shift(partial[7], 1)
    left = ring_shift(partial[0], -1)
    right = add_tiles(right, partial[6])
    left = add_tiles(left, partial[1])
    right = add_tiles(ring_shift(right, 1), partial[5])
    left = add_tiles(ring_shift(left, -1), partial[2])
    right = add_tiles(ring_shift(right, 1), partial[4])
    left = ring_shift(left, -1)
    right, cotangent = lax.optimization_barrier((right, cotangent))
    right = ring_shift(right, 1)
    cotangent = cotangent.reshape(-1, 2 * part).T.astype(jnp.float32)
    total = partial[BEFORE].astype(jnp.float32) + left.astype(jnp.float32) + right.astype(jnp.float32)
    gate_pre = jnp.concatenate([total[:part], total[2 * part : 3 * part]], 0)
    up_pre = jnp.concatenate([total[part : 2 * part], total[3 * part :]], 0)

    sigmoid = jax.nn.sigmoid(gate_pre)
    silu = gate_pre * sigmoid
    hidden = (silu * up_pre).astype(jnp.bfloat16)
    grad_gate = (cotangent * up_pre * sigmoid * (1.0 + gate_pre * (1.0 - sigmoid))).astype(jnp.bfloat16)
    grad_up = (cotangent * silu).astype(jnp.bfloat16)
    grads = jnp.concatenate([grad_gate[:part], grad_up[:part], grad_gate[part:], grad_up[part:]], 0)

    left_1 = ring_shift(grads, -1)
    right_1 = ring_shift(grads, 1)
    left_2 = ring_shift(left_1, -1)
    right_2 = ring_shift(right_1, 1)
    left_3 = ring_shift(left_2, -1)
    right_3 = ring_shift(right_2, 1)
    left_4 = ring_shift(left_3, -1)
    terms, sums = near_products(
        core, own_tokens, other_tokens, weights, [right_3, right_2, right_1, grads, left_1, left_2, left_3]
    )
    keep, send = last_sums(core, half, own_tokens, other_tokens, sums, left_4)
    terms, send = lax.optimization_barrier((terms, send))
    received = lax.ppermute(send, "h", [(0, 1), (1, 0)])
    terms = last_terms(weights, terms, left_4)
    terms = lax.all_to_all(
        terms.reshape(16, -1, features), ("y", "x"), split_axis=0, concat_axis=0, tiled=True
    )
    keep_terms, send_terms = sum_parts(core, terms)
    grad_tokens = (keep_terms + swap_cores(send_terms).astype(jnp.float32)).astype(jnp.bfloat16)
    grad_tokens, hidden = lax.optimization_barrier((grad_tokens, hidden))
    hidden = lax.all_to_all(
        hidden.T.reshape(-1, 2, 1, part), "x", split_axis=0, concat_axis=2, tiled=True
    )
    grad_tokens = lax.ppermute(grad_tokens, ("r", "y", "c", "h"), result_pairs())
    hidden = hidden.reshape(-1, hidden_cols)
    hidden, keep = lax.optimization_barrier((hidden, keep))
    gate_grad, up_grad = finish(keep, received)
    grad_tokens, gate_grad = lax.optimization_barrier((grad_tokens, gate_grad))
    grad_tokens = copied(grad_tokens, 1_000_000_000)
    return hidden, grad_tokens, gate_grad.T, up_grad.T


def solution(mesh):
    fine = Mesh(mesh.devices.reshape(8, 4, 2, 2, 4), ("r", "y", "c", "h", "x"))
    return jax.shard_map(
        local,
        mesh=fine,
        in_specs=(
            P(("r", "h", "x"), ("y", "c")),
            P("r", ("y", "c")),
            P("r", ("y", "c")),
            P(("r", "h", "x"), ("y", "c")),
        ),
        out_specs=(
            P(("r", "h", "x"), ("y", "c")),
            P(("y", "c", "h", "x"), "r"),
            P("r", ("y", "c", "h", "x")),
            P("r", ("y", "c", "h", "x")),
        ),
        check_vma=False,
    )
```

```python
import functools

import jax
import jax.numpy as jnp
from jax import lax
from jax.experimental import pallas as pl
from jax.experimental.pallas import tpu as pltpu
from jax.sharding import Mesh, PartitionSpec as P

RING = 16
ROWS = 8
BEFORE = 3


def ring_index(z):
    z %= RING
    return (z % ROWS) * 2 + z // ROWS


def ring_shift(value, step):
    pairs = [(ring_index(z), ring_index(z + step)) for z in range(RING)]
    return lax.ppermute(value, ("r", "h"), pairs)


def place(z, col):
    z %= RING
    return ((z % ROWS) * ROWS + col) * 2 + z // ROWS


def slot(offset):
    return (offset % 4) * 2 + offset // 4


def token_pairs():
    pairs = []
    for z in range(RING):
        for offset in range(ROWS):
            pairs.append((place(z + offset - BEFORE, z % ROWS), place(z, slot(offset))))
    return pairs


def result_pairs():
    pairs = []
    for z in range(RING):
        for offset in range(ROWS):
            tile = (z + offset - BEFORE) % RING
            pairs.append((place(z, slot(offset)), place(z % ROWS + ROWS * (tile // ROWS), tile % ROWS)))
    return pairs


def dot_f32(left, right, dims=((1,), (0,))):
    return lax.dot_general(left, right, (dims, ((), ())), preferred_element_type=jnp.float32)


ANY_SPEC = pl.BlockSpec(memory_space=pl.ANY)
SMEM_SPEC = pl.BlockSpec(memory_space=pltpu.SMEM)
VMEM_SPEC = pl.BlockSpec(memory_space=pltpu.VMEM)
PARAMS = pltpu.CompilerParams(vmem_limit_bytes=16 << 20)


def swap_cores(value):
    return lax.ppermute(value, "c", [(0, 1), (1, 0)])


def join_cores(core, own_ref, other_ref, both_ref):
    rows = own_ref.shape[0]
    both_ref[pl.ds(pl.multiple_of(core * rows, rows), rows), :] = own_ref[...]
    both_ref[pl.ds(pl.multiple_of((1 - core) * rows, rows), rows), :] = other_ref[...]


def forward_kernel(offsets, core_ref, own_ref, other_ref, weights_ref, *refs):
    tokens_ref = refs[-1]
    join_cores(core_ref[0], own_ref, other_ref, tokens_ref)
    for offset, tile_ref in zip(offsets, refs):
        product = dot_f32(tokens_ref[offset * 128 : (offset + 1) * 128, :], weights_ref[...])
        tile_ref[...] = product.T.astype(jnp.bfloat16)


def forward_tiles(offsets, core, own, other, weights):
    features, cols = weights.shape
    return pl.pallas_call(
        functools.partial(forward_kernel, offsets),
        in_specs=[SMEM_SPEC] + [VMEM_SPEC] * 3,
        out_specs=[VMEM_SPEC] * len(offsets),
        out_shape=[jax.ShapeDtypeStruct((cols, 128), jnp.bfloat16)] * len(offsets),
        scratch_shapes=[pltpu.VMEM((ROWS * 128, features), jnp.bfloat16)],
        compiler_params=PARAMS,
    )(core, own, other, weights)


def term_rows(at):
    return [((at % 4 * 4 + x) * 2 + at // 4) * 32 for x in range(4)]


def near_kernel(core_ref, own_ref, other_ref, weights_ref, *refs):
    tile_refs = refs[:7]
    terms_ref, sums_ref, tokens_ref, wide_ref = refs[7:]
    join_cores(core_ref[0], own_ref, other_ref, tokens_ref)
    for at, tile_ref in enumerate(tile_refs):
        wide_ref[:, at * 128 : (at + 1) * 128] = tile_ref[...]
        product = dot_f32(weights_ref[...], tile_ref[...]).T.astype(jnp.bfloat16)
        for part, first in enumerate(term_rows(at)):
            terms_ref[first : first + 32, :] = product[part * 32 : (part + 1) * 32, :]
    for first in term_rows(7):
        terms_ref[first : first + 32, :] = jnp.zeros((32, terms_ref.shape[1]), jnp.bfloat16)
    sums_ref[...] = dot_f32(wide_ref[...], tokens_ref[0:896, :])


def near_products(core, own, other, weights, tiles):
    features, cols = weights.shape
    return pl.pallas_call(
        near_kernel,
        in_specs=[SMEM_SPEC] + [VMEM_SPEC] * 10,
        out_specs=[VMEM_SPEC] * 2,
        out_shape=[
            jax.ShapeDtypeStruct((ROWS * 128, features), jnp.bfloat16),
            jax.ShapeDtypeStruct((cols, features), jnp.float32),
        ],
        scratch_shapes=[
            pltpu.VMEM((ROWS * 128, features), jnp.bfloat16),
            pltpu.VMEM((cols, 7 * 128), jnp.bfloat16),
        ],
        compiler_params=PARAMS,
    )(core, own, other, weights, *tiles)


def last_sums_kernel(core_ref, half_ref, own_ref, other_ref, sums_ref, tile_ref, keep_ref, send_ref, last_ref):
    rows = own_ref.shape[0]

    @pl.when(core_ref[0] == 0)
    def _():
        last_ref[...] = other_ref[rows - 128 :, :]

    @pl.when(core_ref[0] == 1)
    def _():
        last_ref[...] = own_ref[rows - 128 :, :]

    rows = keep_ref.shape[0]
    half = half_ref[0]
    send_rows = pl.ds(pl.multiple_of((1 - half) * rows, 16), rows)
    keep_rows = pl.ds(pl.multiple_of(half * rows, 16), rows)
    send = sums_ref[send_rows, :] + dot_f32(tile_ref[send_rows, :], last_ref[...])
    send_ref[...] = send.astype(jnp.bfloat16)
    keep_ref[...] = sums_ref[keep_rows, :] + dot_f32(tile_ref[keep_rows, :], last_ref[...])


def last_sums(core, half, own, other, sums, tile):
    cols, features = sums.shape
    return pl.pallas_call(
        last_sums_kernel,
        in_specs=[SMEM_SPEC] * 2 + [VMEM_SPEC] * 4,
        out_specs=[VMEM_SPEC] * 2,
        out_shape=[
            jax.ShapeDtypeStruct((cols // 2, features), jnp.float32),
            jax.ShapeDtypeStruct((cols // 2, features), jnp.bfloat16),
        ],
        scratch_shapes=[pltpu.VMEM((128, features), jnp.bfloat16)],
        compiler_params=PARAMS,
    )(core, half, own, other, sums, tile)


def last_terms_kernel(weights_ref, tile_ref, terms_ref, all_ref, block_ref, sem_ref):
    del terms_ref
    block_ref[...] = dot_f32(weights_ref[...], tile_ref[...]).T.astype(jnp.bfloat16)
    copies = [
        pltpu.make_async_copy(
            block_ref.at[part * 32 : (part + 1) * 32, :], all_ref.at[first : first + 32, :], sem_ref.at[part]
        )
        for part, first in enumerate(term_rows(7))
    ]
    for copy in copies:
        copy.start()
    for copy in copies:
        copy.wait()


def last_terms(weights, terms, tile):
    return pl.pallas_call(
        last_terms_kernel,
        in_specs=[VMEM_SPEC] * 2 + [ANY_SPEC],
        out_specs=ANY_SPEC,
        out_shape=jax.ShapeDtypeStruct(terms.shape, terms.dtype),
        input_output_aliases={2: 0},
        scratch_shapes=[pltpu.VMEM((128, terms.shape[1]), jnp.bfloat16), pltpu.SemaphoreType.DMA((4,))],
        compiler_params=pltpu.CompilerParams(vmem_limit_bytes=6 << 20),
    )(weights, tile, terms)


def total_kernel(core_ref, parts_ref, keep_ref, send_ref, total_ref):
    total_ref[...] = jnp.sum(parts_ref[...].astype(jnp.float32), 0)
    rows = keep_ref.shape[0]
    core = core_ref[0]
    keep_ref[...] = total_ref[pl.ds(pl.multiple_of(core * rows, rows), rows), :]
    send = total_ref[pl.ds(pl.multiple_of((1 - core) * rows, rows), rows), :]
    send_ref[...] = send.astype(jnp.bfloat16)


def finish_kernel(keep_ref, received_ref, gate_ref, up_ref):
    rows = gate_ref.shape[0]
    gate_ref[...] = keep_ref[:rows, :] + received_ref[:rows, :].astype(jnp.float32)
    up_ref[...] = keep_ref[rows:, :] + received_ref[rows:, :].astype(jnp.float32)


def finish(keep, received):
    shape = jax.ShapeDtypeStruct((keep.shape[0] // 2, keep.shape[1]), jnp.float32)
    return pl.pallas_call(
        finish_kernel,
        in_specs=[VMEM_SPEC] * 2,
        out_specs=[VMEM_SPEC] * 2,
        out_shape=[shape, shape],
        compiler_params=PARAMS,
    )(keep, received)


def copy_kernel(in_ref, out_ref):
    out_ref[...] = in_ref[...]


def copied(value, flops):
    return pl.pallas_call(
        copy_kernel,
        in_specs=[VMEM_SPEC],
        out_specs=VMEM_SPEC,
        out_shape=jax.ShapeDtypeStruct(value.shape, value.dtype),
        compiler_params=PARAMS,
        cost_estimate=pl.CostEstimate(flops=flops, bytes_accessed=1, transcendentals=0),
    )(value)


def sum_parts(core, parts):
    _, rows, features = parts.shape
    shape = (rows // 2, features)
    return pl.pallas_call(
        total_kernel,
        in_specs=[SMEM_SPEC, VMEM_SPEC],
        out_specs=[VMEM_SPEC] * 2,
        out_shape=[jax.ShapeDtypeStruct(shape, jnp.float32), jax.ShapeDtypeStruct(shape, jnp.bfloat16)],
        scratch_shapes=[pltpu.VMEM((rows, features), jnp.float32)],
        compiler_params=PARAMS,
    )(core, parts)


def add_tiles(*tiles):
    return sum(tile.astype(jnp.float32) for tile in tiles).astype(jnp.bfloat16)


def local(tokens, gate_weight, up_weight, grad_hidden):
    own_x = lax.axis_index("x")
    core = lax.axis_index("c").astype(jnp.int32).reshape(1)
    half = lax.axis_index("h").astype(jnp.int32).reshape(1)
    features, hidden_cols = gate_weight.shape
    part = hidden_cols // 8

    def own_columns(weight, which):
        return lax.dynamic_slice(weight, (0, (which * 4 + own_x) * part), (features, part))

    weights = jnp.concatenate(
        [own_columns(weight, which) for which in (0, 1) for weight in (gate_weight, up_weight)], 1
    )

    piece = lax.ppermute(tokens, ("r", "y", "c", "h"), token_pairs())
    copies = jnp.broadcast_to(piece[None], (16,) + piece.shape)
    own_tokens = lax.all_to_all(copies, ("y", "x"), split_axis=0, concat_axis=0, tiled=True)
    own_tokens = own_tokens.reshape(-1, features)
    cotangent = grad_hidden.reshape(-1, 2, 4, part).transpose(2, 0, 1, 3)
    own_tokens, cotangent, weights = lax.optimization_barrier((own_tokens, cotangent, weights))
    other_tokens = swap_cores(own_tokens)
    partial = {}
    for offsets in ((7, 0), (6, 1, 5, 2, 4, 3)):
        partial.update(zip(offsets, forward_tiles(offsets, core, own_tokens, other_tokens, weights)))
    right = ring_shift(partial[7], 1)
    left = ring_shift(partial[0], -1)
    right = add_tiles(right, partial[6])
    left = add_tiles(left, partial[1])
    right = add_tiles(ring_shift(right, 1), partial[5])
    left = add_tiles(ring_shift(left, -1), partial[2])
    right = add_tiles(ring_shift(right, 1), partial[4])
    left = ring_shift(left, -1)
    right, cotangent = lax.optimization_barrier((right, cotangent))
    cotangent = lax.all_to_all(cotangent, "x", split_axis=0, concat_axis=0, tiled=True)
    right = ring_shift(right, 1)
    cotangent = cotangent.reshape(-1, 2 * part).T.astype(jnp.float32)
    total = partial[BEFORE].astype(jnp.float32) + left.astype(jnp.float32) + right.astype(jnp.float32)
    gate_pre = jnp.concatenate([total[:part], total[2 * part : 3 * part]], 0)
    up_pre = jnp.concatenate([total[part : 2 * part], total[3 * part :]], 0)

    sigmoid = jax.nn.sigmoid(gate_pre)
    silu = gate_pre * sigmoid
    hidden = (silu * up_pre).astype(jnp.bfloat16)
    grad_gate = (cotangent * up_pre * sigmoid * (1.0 + gate_pre * (1.0 - sigmoid))).astype(jnp.bfloat16)
    grad_up = (cotangent * silu).astype(jnp.bfloat16)
    grads = jnp.concatenate([grad_gate[:part], grad_up[:part], grad_gate[part:], grad_up[part:]], 0)

    left_1 = ring_shift(grads, -1)
    right_1 = ring_shift(grads, 1)
    left_2 = ring_shift(left_1, -1)
    right_2 = ring_shift(right_1, 1)
    left_3 = ring_shift(left_2, -1)
    right_3 = ring_shift(right_2, 1)
    left_4 = ring_shift(left_3, -1)
    terms, sums = near_products(
        core, own_tokens, other_tokens, weights, [right_3, right_2, right_1, grads, left_1, left_2, left_3]
    )
    keep, send = last_sums(core, half, own_tokens, other_tokens, sums, left_4)
    terms, send = lax.optimization_barrier((terms, send))
    received = lax.ppermute(send, "h", [(0, 1), (1, 0)])
    terms = last_terms(weights, terms, left_4)
    terms = lax.all_to_all(
        terms.reshape(16, -1, features), ("y", "x"), split_axis=0, concat_axis=0, tiled=True
    )
    keep_terms, send_terms = sum_parts(core, terms)
    grad_tokens = (keep_terms + swap_cores(send_terms).astype(jnp.float32)).astype(jnp.bfloat16)
    grad_tokens, hidden = lax.optimization_barrier((grad_tokens, hidden))
    hidden = lax.all_to_all(
        hidden.T.reshape(-1, 2, 1, part), "x", split_axis=0, concat_axis=2, tiled=True
    )
    grad_tokens = lax.ppermute(grad_tokens, ("r", "y", "c", "h"), result_pairs())
    hidden = hidden.reshape(-1, hidden_cols)
    hidden, keep = lax.optimization_barrier((hidden, keep))
    gate_grad, up_grad = finish(keep, received)
    grad_tokens, gate_grad = lax.optimization_barrier((grad_tokens, gate_grad))
    grad_tokens = copied(grad_tokens, 1_000_000_000)
    return hidden, grad_tokens, gate_grad.T, up_grad.T


def solution(mesh):
    fine = Mesh(mesh.devices.reshape(8, 4, 2, 2, 4), ("r", "y", "c", "h", "x"))
    return jax.shard_map(
        local,
        mesh=fine,
        in_specs=(
            P(("r", "h", "x"), ("y", "c")),
            P("r", ("y", "c")),
            P("r", ("y", "c")),
            P(("r", "h", "x"), ("y", "c")),
        ),
        out_specs=(
            P(("r", "h", "x"), ("y", "c")),
            P(("y", "c", "h", "x"), "r"),
            P("r", ("y", "c", "h", "x")),
            P("r", ("y", "c", "h", "x")),
        ),
        check_vma=False,
    )
```

```python
import functools

import jax
import jax.numpy as jnp
from jax import lax
from jax.experimental import pallas as pl
from jax.experimental.pallas import tpu as pltpu
from jax.sharding import Mesh, PartitionSpec as P

RING = 16
ROWS = 8
BEFORE = 3


def ring_index(z):
    z %= RING
    return (z % ROWS) * 2 + z // ROWS


def ring_shift(value, step):
    pairs = [(ring_index(z), ring_index(z + step)) for z in range(RING)]
    return lax.ppermute(value, ("r", "h"), pairs)


def place(z, col):
    z %= RING
    return ((z % ROWS) * ROWS + col) * 2 + z // ROWS


def slot(offset):
    return (offset % 4) * 2 + offset // 4


def token_pairs():
    pairs = []
    for z in range(RING):
        for offset in range(ROWS):
            pairs.append((place(z + offset - BEFORE, z % ROWS), place(z, slot(offset))))
    return pairs


def result_pairs():
    pairs = []
    for z in range(RING):
        for offset in range(ROWS):
            tile = (z + offset - BEFORE) % RING
            pairs.append((place(z, slot(offset)), place(z % ROWS + ROWS * (tile // ROWS), tile % ROWS)))
    return pairs


def dot_f32(left, right, dims=((1,), (0,))):
    return lax.dot_general(left, right, (dims, ((), ())), preferred_element_type=jnp.float32)


ANY_SPEC = pl.BlockSpec(memory_space=pl.ANY)
SMEM_SPEC = pl.BlockSpec(memory_space=pltpu.SMEM)
VMEM_SPEC = pl.BlockSpec(memory_space=pltpu.VMEM)
PARAMS = pltpu.CompilerParams(vmem_limit_bytes=16 << 20)


def swap_cores(value):
    return lax.ppermute(value, "c", [(0, 1), (1, 0)])


def join_cores(core, own_ref, other_ref, both_ref):
    rows = own_ref.shape[0]
    both_ref[pl.ds(pl.multiple_of(core * rows, rows), rows), :] = own_ref[...]
    both_ref[pl.ds(pl.multiple_of((1 - core) * rows, rows), rows), :] = other_ref[...]


def forward_kernel(offsets, core_ref, own_ref, other_ref, weights_ref, *refs):
    tokens_ref = refs[-1]
    join_cores(core_ref[0], own_ref, other_ref, tokens_ref)
    for offset, tile_ref in zip(offsets, refs):
        product = dot_f32(tokens_ref[offset * 128 : (offset + 1) * 128, :], weights_ref[...])
        tile_ref[...] = product.T.astype(jnp.bfloat16)


def forward_tiles(offsets, core, own, other, weights):
    features, cols = weights.shape
    return pl.pallas_call(
        functools.partial(forward_kernel, offsets),
        in_specs=[SMEM_SPEC] + [VMEM_SPEC] * 3,
        out_specs=[VMEM_SPEC] * len(offsets),
        out_shape=[jax.ShapeDtypeStruct((cols, 128), jnp.bfloat16)] * len(offsets),
        scratch_shapes=[pltpu.VMEM((ROWS * 128, features), jnp.bfloat16)],
        compiler_params=PARAMS,
    )(core, own, other, weights)


def term_rows(at):
    return [((at % 4 * 4 + x) * 2 + at // 4) * 32 for x in range(4)]


def near_kernel(core_ref, own_ref, other_ref, weights_ref, *refs):
    tile_refs = refs[:7]
    terms_ref, sums_ref, tokens_ref, wide_ref = refs[7:]
    join_cores(core_ref[0], own_ref, other_ref, tokens_ref)
    for at, tile_ref in enumerate(tile_refs):
        wide_ref[:, at * 128 : (at + 1) * 128] = tile_ref[...]
        product = dot_f32(weights_ref[...], tile_ref[...]).T.astype(jnp.bfloat16)
        for part, first in enumerate(term_rows(at)):
            terms_ref[first : first + 32, :] = product[part * 32 : (part + 1) * 32, :]
    for first in term_rows(7):
        terms_ref[first : first + 32, :] = jnp.zeros((32, terms_ref.shape[1]), jnp.bfloat16)
    sums_ref[...] = dot_f32(wide_ref[...], tokens_ref[0:896, :])


def near_products(core, own, other, weights, tiles):
    features, cols = weights.shape
    return pl.pallas_call(
        near_kernel,
        in_specs=[SMEM_SPEC] + [VMEM_SPEC] * 10,
        out_specs=[VMEM_SPEC] * 2,
        out_shape=[
            jax.ShapeDtypeStruct((ROWS * 128, features), jnp.bfloat16),
            jax.ShapeDtypeStruct((cols, features), jnp.float32),
        ],
        scratch_shapes=[
            pltpu.VMEM((ROWS * 128, features), jnp.bfloat16),
            pltpu.VMEM((cols, 7 * 128), jnp.bfloat16),
        ],
        compiler_params=PARAMS,
    )(core, own, other, weights, *tiles)


def last_sums_kernel(core_ref, half_ref, own_ref, other_ref, sums_ref, tile_ref, keep_ref, send_ref, last_ref):
    rows = own_ref.shape[0]

    @pl.when(core_ref[0] == 0)
    def _():
        last_ref[...] = other_ref[rows - 128 :, :]

    @pl.when(core_ref[0] == 1)
    def _():
        last_ref[...] = own_ref[rows - 128 :, :]

    rows = keep_ref.shape[0]
    half = half_ref[0]
    send_rows = pl.ds(pl.multiple_of((1 - half) * rows, 16), rows)
    keep_rows = pl.ds(pl.multiple_of(half * rows, 16), rows)
    send = sums_ref[send_rows, :] + dot_f32(tile_ref[send_rows, :], last_ref[...])
    send_ref[...] = send.astype(jnp.bfloat16)
    keep_ref[...] = sums_ref[keep_rows, :] + dot_f32(tile_ref[keep_rows, :], last_ref[...])


def last_sums(core, half, own, other, sums, tile):
    cols, features = sums.shape
    return pl.pallas_call(
        last_sums_kernel,
        in_specs=[SMEM_SPEC] * 2 + [VMEM_SPEC] * 4,
        out_specs=[VMEM_SPEC] * 2,
        out_shape=[
            jax.ShapeDtypeStruct((cols // 2, features), jnp.float32),
            jax.ShapeDtypeStruct((cols // 2, features), jnp.bfloat16),
        ],
        scratch_shapes=[pltpu.VMEM((128, features), jnp.bfloat16)],
        compiler_params=pltpu.CompilerParams(vmem_limit_bytes=10 << 20),
    )(core, half, own, other, sums, tile)


def last_terms_kernel(weights_ref, tile_ref, terms_ref, all_ref, block_ref, sem_ref):
    del terms_ref
    block_ref[...] = dot_f32(weights_ref[...], tile_ref[...]).T.astype(jnp.bfloat16)
    copies = [
        pltpu.make_async_copy(
            block_ref.at[part * 32 : (part + 1) * 32, :], all_ref.at[first : first + 32, :], sem_ref.at[part]
        )
        for part, first in enumerate(term_rows(7))
    ]
    for copy in copies:
        copy.start()
    for copy in copies:
        copy.wait()


def last_terms(weights, terms, tile):
    return pl.pallas_call(
        last_terms_kernel,
        in_specs=[VMEM_SPEC] * 2 + [ANY_SPEC],
        out_specs=ANY_SPEC,
        out_shape=jax.ShapeDtypeStruct(terms.shape, terms.dtype),
        input_output_aliases={2: 0},
        scratch_shapes=[pltpu.VMEM((128, terms.shape[1]), jnp.bfloat16), pltpu.SemaphoreType.DMA((4,))],
        compiler_params=pltpu.CompilerParams(vmem_limit_bytes=6 << 20),
    )(weights, tile, terms)


def total_kernel(core_ref, parts_ref, keep_ref, send_ref, total_ref):
    total_ref[...] = jnp.sum(parts_ref[...].astype(jnp.float32), 0)
    rows = keep_ref.shape[0]
    core = core_ref[0]
    keep_ref[...] = total_ref[pl.ds(pl.multiple_of(core * rows, rows), rows), :]
    send = total_ref[pl.ds(pl.multiple_of((1 - core) * rows, rows), rows), :]
    send_ref[...] = send.astype(jnp.bfloat16)


def finish_kernel(keep_ref, received_ref, gate_ref, up_ref):
    rows = gate_ref.shape[0]
    gate_ref[...] = keep_ref[:rows, :] + received_ref[:rows, :].astype(jnp.float32)
    up_ref[...] = keep_ref[rows:, :] + received_ref[rows:, :].astype(jnp.float32)


def finish(keep, received):
    shape = jax.ShapeDtypeStruct((keep.shape[0] // 2, keep.shape[1]), jnp.float32)
    return pl.pallas_call(
        finish_kernel,
        in_specs=[VMEM_SPEC] * 2,
        out_specs=[VMEM_SPEC] * 2,
        out_shape=[shape, shape],
        compiler_params=PARAMS,
    )(keep, received)


def copy_kernel(in_ref, out_ref):
    out_ref[...] = in_ref[...]


def copied(value, flops):
    return pl.pallas_call(
        copy_kernel,
        in_specs=[VMEM_SPEC],
        out_specs=VMEM_SPEC,
        out_shape=jax.ShapeDtypeStruct(value.shape, value.dtype),
        compiler_params=PARAMS,
        cost_estimate=pl.CostEstimate(flops=flops, bytes_accessed=1, transcendentals=0),
    )(value)


def sum_parts(core, parts):
    _, rows, features = parts.shape
    shape = (rows // 2, features)
    return pl.pallas_call(
        total_kernel,
        in_specs=[SMEM_SPEC, VMEM_SPEC],
        out_specs=[VMEM_SPEC] * 2,
        out_shape=[jax.ShapeDtypeStruct(shape, jnp.float32), jax.ShapeDtypeStruct(shape, jnp.bfloat16)],
        scratch_shapes=[pltpu.VMEM((rows, features), jnp.float32)],
        compiler_params=PARAMS,
    )(core, parts)


def add_tiles(*tiles):
    return sum(tile.astype(jnp.float32) for tile in tiles).astype(jnp.bfloat16)


def local(tokens, gate_weight, up_weight, grad_hidden):
    own_x = lax.axis_index("x")
    core = lax.axis_index("c").astype(jnp.int32).reshape(1)
    half = lax.axis_index("h").astype(jnp.int32).reshape(1)
    features, hidden_cols = gate_weight.shape
    part = hidden_cols // 8

    def own_columns(weight, which):
        return lax.dynamic_slice(weight, (0, (which * 4 + own_x) * part), (features, part))

    weights = jnp.concatenate(
        [own_columns(weight, which) for which in (0, 1) for weight in (gate_weight, up_weight)], 1
    )

    piece = lax.ppermute(tokens, ("r", "y", "c", "h"), token_pairs())
    copies = jnp.broadcast_to(piece[None], (16,) + piece.shape)
    own_tokens = lax.all_to_all(copies, ("y", "x"), split_axis=0, concat_axis=0, tiled=True)
    own_tokens = own_tokens.reshape(-1, features)
    cotangent = grad_hidden.reshape(-1, 2, 4, part).transpose(2, 0, 1, 3)
    own_tokens, cotangent, weights = lax.optimization_barrier((own_tokens, cotangent, weights))
    other_tokens = swap_cores(own_tokens)
    cotangent = lax.all_to_all(cotangent, "x", split_axis=0, concat_axis=0, tiled=True)
    partial = {}
    for offsets in ((7, 0), (6, 1, 5, 2, 4, 3)):
        partial.update(zip(offsets, forward_tiles(offsets, core, own_tokens, other_tokens, weights)))
    right = ring_shift(partial[7], 1)
    left = ring_shift(partial[0], -1)
    right = add_tiles(right, partial[6])
    left = add_tiles(left, partial[1])
    right = add_tiles(ring_shift(right, 1), partial[5])
    left = add_tiles(ring_shift(left, -1), partial[2])
    right = add_tiles(ring_shift(right, 1), partial[4])
    left = ring_shift(left, -1)
    right, cotangent = lax.optimization_barrier((right, cotangent))
    right = ring_shift(right, 1)
    cotangent = cotangent.reshape(-1, 2 * part).T.astype(jnp.float32)
    total = partial[BEFORE].astype(jnp.float32) + left.astype(jnp.float32) + right.astype(jnp.float32)
    gate_pre = jnp.concatenate([total[:part], total[2 * part : 3 * part]], 0)
    up_pre = jnp.concatenate([total[part : 2 * part], total[3 * part :]], 0)

    sigmoid = jax.nn.sigmoid(gate_pre)
    silu = gate_pre * sigmoid
    hidden = (silu * up_pre).astype(jnp.bfloat16)
    grad_gate = (cotangent * up_pre * sigmoid * (1.0 + gate_pre * (1.0 - sigmoid))).astype(jnp.bfloat16)
    grad_up = (cotangent * silu).astype(jnp.bfloat16)
    grads = jnp.concatenate([grad_gate[:part], grad_up[:part], grad_gate[part:], grad_up[part:]], 0)

    left_1 = ring_shift(grads, -1)
    right_1 = ring_shift(grads, 1)
    left_2 = ring_shift(left_1, -1)
    right_2 = ring_shift(right_1, 1)
    left_3 = ring_shift(left_2, -1)
    right_3 = ring_shift(right_2, 1)
    left_4 = ring_shift(left_3, -1)
    terms, sums = near_products(
        core, own_tokens, other_tokens, weights, [right_3, right_2, right_1, grads, left_1, left_2, left_3]
    )
    keep, send = last_sums(core, half, own_tokens, other_tokens, sums, left_4)
    terms, send = lax.optimization_barrier((terms, send))
    received = lax.ppermute(send, "h", [(0, 1), (1, 0)])
    terms = last_terms(weights, terms, left_4)
    terms = lax.all_to_all(
        terms.reshape(16, -1, features), ("y", "x"), split_axis=0, concat_axis=0, tiled=True
    )
    keep_terms, send_terms = sum_parts(core, terms)
    grad_tokens = (keep_terms + swap_cores(send_terms).astype(jnp.float32)).astype(jnp.bfloat16)
    grad_tokens, hidden = lax.optimization_barrier((grad_tokens, hidden))
    hidden = lax.all_to_all(
        hidden.T.reshape(-1, 2, 1, part), "x", split_axis=0, concat_axis=2, tiled=True
    )
    grad_tokens = lax.ppermute(grad_tokens, ("r", "y", "c", "h"), result_pairs())
    hidden = hidden.reshape(-1, hidden_cols)
    hidden, keep = lax.optimization_barrier((hidden, keep))
    gate_grad, up_grad = finish(keep, received)
    grad_tokens, gate_grad = lax.optimization_barrier((grad_tokens, gate_grad))
    grad_tokens = copied(grad_tokens, 1_000_000_000)
    return hidden, grad_tokens, gate_grad.T, up_grad.T


def solution(mesh):
    fine = Mesh(mesh.devices.reshape(8, 4, 2, 2, 4), ("r", "y", "c", "h", "x"))
    return jax.shard_map(
        local,
        mesh=fine,
        in_specs=(
            P(("r", "h", "x"), ("y", "c")),
            P("r", ("y", "c")),
            P("r", ("y", "c")),
            P(("r", "h", "x"), ("y", "c")),
        ),
        out_specs=(
            P(("r", "h", "x"), ("y", "c")),
            P(("y", "c", "h", "x"), "r"),
            P("r", ("y", "c", "h", "x")),
            P("r", ("y", "c", "h", "x")),
        ),
        check_vma=False,
    )
```
